256 devices in a mesh: loop: 64 (over z, x_hi, y), depth: 4 (over x_lo, core).
Axes of the slice: x: 4 (x_hi: 2, x_lo: 2; x = x_hi * 2 + x_lo), y: 4, z: 8, core: 2. Of those that a mesh axis runs over, the one named last changes fastest.
Arguments:
- features: float32 [65536, 128], P(('loop', 'depth')), may hold values from -6 to 6
- norm_scale: float32 [65536], P(('loop', 'depth')), may hold values from 0.03 to 0.3
- weight: bfloat16 [128, 128], replicated, may hold values from -0.5 to 0.5
- cotangent: float32 [65536, 128], P(('loop', 'depth')), may hold values from -6 to 6
- tile_rows: int32 [64, 4, 16, 48], P('loop', 'depth'), may hold values from 0 to 7
- tile_cols: int32 [64, 4, 16, 48], P('loop', 'depth'), may hold values from 0 to 7
- tile_masks: int32 [64, 4, 16, 48, 2048], P('loop', 'depth'), may hold values from 0 to 255, as said below
- tile_counts: int32 [64, 4, 16], P('loop', 'depth'), may hold values from 1 to 48, as said below
Outputs:
- activations: float32 [65536, 128], P(('loop', 'depth'))
- feature_grad: float32 [65536, 128], P(('loop', 'depth'))
- weight_grad: float32 [128, 128], replicated
The draws below stay inside these ranges and needn't reach their ends.
Inputs may be any that keep to these rules, and one draw needn't show every extreme that they name: `tile_rows`: tile row inside the target block row. `tile_cols`: tile column inside the source block row. `tile_masks`: each word packs 8 entries of a tile row. Slots from tile_counts on are unused. Some block row, member and section uses all 48 slots in every draw.
All inputs are finite; a program needn't handle non-finite values.
Results may differ from the reference program's by a relative error of at most 0.0057.
Values may be sent and summed in bfloat16 or wider, within the bound.
A program may use at most 64 MiB of HBM per device.

```python
import math
import jax
import jax.numpy as jnp
from jax import lax

FEAT = 128
TILE = 128
CAP = 48
WORDS = 16
STRIPES = 64
COPIES = 4
SECTIONS = 16
STRIPE_TILES = 8
NODES = 65536


def draw_tile_counts(key, part):
    key = jax.random.fold_in(key, 7)
    key_heat, key_cut, key_stripe, key_member, key_section = jax.random.split(key, 5)
    heat_level = jax.random.randint(key_heat, (STRIPES, COPIES, 1), 1, 5)
    cut_amount = jax.random.randint(key_cut, (STRIPES, COPIES, SECTIONS), 0, CAP // 4 + 1)
    counts = jnp.clip(CAP * heat_level // 4 - cut_amount, 1, CAP)
    stripe_pick = jax.random.randint(key_stripe, (), 0, STRIPES)
    member_pick = jax.random.randint(key_member, (), 0, COPIES)
    section_pick = jax.random.randint(key_section, (), 0, SECTIONS)
    counts = counts.at[stripe_pick, member_pick, section_pick].set(CAP)
    return counts.astype(jnp.int32)


def draw_tile_masks(key, part):
    key = jax.random.fold_in(key, 11)
    keys = jax.random.split(key, 8)
    shape = (STRIPES, COPIES, SECTIONS, CAP, TILE * WORDS)
    level = jax.random.randint(keys[0], (STRIPES, COPIES, SECTIONS, CAP, 1), 0, 3)
    words = jax.random.randint(keys[1], shape, 0, 256)
    for index in range(2, 6):
        words = jnp.bitwise_and(words, jax.random.randint(keys[index], shape, 0, 256))
    extra_one = jnp.where(level >= 1, jax.random.randint(keys[6], shape, 0, 256), 255)
    extra_two = jnp.where(level >= 2, jax.random.randint(keys[7], shape, 0, 256), 255)
    words = jnp.bitwise_and(words, jnp.bitwise_and(extra_one, extra_two))
    return words.astype(jnp.int32)


def touch_ends(values, key, least, largest):
    place = [jax.random.randint(jax.random.fold_in(key, axis), (), 0, length) for axis, length in enumerate(values.shape)]
    longest = values.shape.index(max(values.shape))
    neighbour = place[:longest] + [(place[longest] + 1) % values.shape[longest]] + place[longest + 1:]
    return values.at[tuple(place)].set(least).at[tuple(neighbour)].set(largest)


def levels(own_key, dims, cuts, low, top_value):
    def one(dim, shards_of):
        steps = jax.random.uniform(jax.random.fold_in(jax.random.fold_in(own_key, 6), dim), (shards_of,), jnp.float32, low / len(cuts), top_value / len(cuts))
        return jnp.repeat(jnp.exp(steps), dims[dim] // shards_of).reshape((-1,) + (1,) * (len(dims) - dim - 1))

    gain = one(*cuts[0])
    for cut in cuts[1:]:
        gain = gain * one(*cut)
    return gain


def noise(rng, dims, scale, limit, pieces=(), kind=jnp.bfloat16):
    entries = scale * jax.random.normal(rng, dims, jnp.float32)
    if pieces:
        entries = entries * levels(rng, dims, pieces, -0.22, 0.18)
    return jnp.clip(entries, -limit, limit).astype(kind)


def setup_inputs(seed: int = 0) -> dict:
    arg_keys = jax.random.split(jax.random.key(seed), 9)
    features = noise(arg_keys[0], (NODES, FEAT), 1.0, 6.0, ((0, 256),), jnp.float32)
    norm_scale = jnp.clip(jnp.exp(math.log(0.3) - 2.3025852 * jax.random.uniform(arg_keys[1], (NODES,), jnp.float32) ** levels(arg_keys[1], (NODES,), ((0, 256),), -0.2, 0.2)), 0.03, 0.3)
    weight = noise(arg_keys[2], (FEAT, FEAT), FEAT ** -0.5, 0.5)
    cotangent = noise(arg_keys[3], (NODES, FEAT), 1.0, 6.0, ((0, 256),), jnp.float32)
    tile_rows = touch_ends(jax.random.randint(arg_keys[4], (STRIPES, COPIES, SECTIONS, CAP), 0, STRIPE_TILES), jax.random.fold_in(arg_keys[4], 1), 0, STRIPE_TILES - 1).astype(jnp.int32)
    tile_cols = touch_ends(jax.random.randint(arg_keys[5], (STRIPES, COPIES, SECTIONS, CAP), 0, STRIPE_TILES), jax.random.fold_in(arg_keys[5], 1), 0, STRIPE_TILES - 1).astype(jnp.int32)
    tile_masks = draw_tile_masks(jax.random.fold_in(arg_keys[8], 71), 0)
    tile_counts = draw_tile_counts(jax.random.fold_in(arg_keys[8], 71), 0)
    return {"features": features, "norm_scale": norm_scale, "weight": weight, "cotangent": cotangent, "tile_rows": tile_rows, "tile_cols": tile_cols, "tile_masks": tile_masks, "tile_counts": tile_counts}


def unpack_bits(words):
    grouped = words.reshape(words.shape[:-1] + (TILE, words.shape[-1] // TILE))
    shifts = jnp.arange(8, dtype=jnp.int32)
    bit_values = jnp.bitwise_and(jnp.right_shift(grouped[..., None], shifts), 1)
    return bit_values.reshape(grouped.shape[:-1] + (grouped.shape[-1] * 8,))


def tile_setup(flat_index, tile_rows, tile_cols, tile_masks, tile_counts):
    stripe_id = flat_index // COPIES
    member_id = flat_index % COPIES
    row_list = tile_rows[stripe_id, member_id]
    col_list = tile_cols[stripe_id, member_id]
    live_slots = jnp.arange(CAP, dtype=jnp.int32)[None, :] < tile_counts[stripe_id, member_id][:, None]
    mask_tiles = unpack_bits(tile_masks[stripe_id, member_id]).astype(jnp.float32)
    mask_tiles = mask_tiles * live_slots[:, :, None, None].astype(jnp.float32)
    source_ids = (stripe_id - member_id - COPIES * jnp.arange(SECTIONS, dtype=jnp.int32)) % STRIPES
    return stripe_id, row_list, col_list, mask_tiles, source_ids.astype(jnp.int32)


def reference(features, norm_scale, weight, cotangent, tile_rows, tile_cols, tile_masks, tile_counts):
    scaled = (norm_scale[:, None] * features).astype(jnp.bfloat16)
    source_tiles = scaled.reshape(STRIPES, STRIPE_TILES, TILE, FEAT)
    flat_ids = jnp.arange(STRIPES * COPIES, dtype=jnp.int32)
    tile_ids = jnp.arange(STRIPE_TILES, dtype=jnp.int32)

    def forward_step(totals, flat_index):
        stripe_id, row_list, col_list, mask_tiles, source_ids = tile_setup(flat_index, tile_rows, tile_cols, tile_masks, tile_counts)
        picked = source_tiles[source_ids[:, None], col_list].astype(jnp.float32)
        products = jnp.einsum("kcij,kcjf->kcif", mask_tiles, picked)
        onehot = (row_list[..., None] == tile_ids).astype(jnp.float32)
        partial_sum = jnp.einsum("kcr,kcif->rif", onehot, products)
        return totals.at[stripe_id].add(partial_sum), None

    empty = jnp.zeros((STRIPES, STRIPE_TILES, TILE, FEAT), jnp.float32)
    summed = lax.scan(forward_step, empty, flat_ids)[0]
    aggregated = norm_scale[:, None] * summed.reshape(NODES, FEAT)
    aggregated_b = aggregated.astype(jnp.bfloat16)
    pre = jnp.dot(aggregated_b, weight, preferred_element_type=jnp.float32)
    activations = jax.nn.silu(pre)
    sigma = jax.nn.sigmoid(pre)
    signal = (cotangent * (sigma * (1.0 + pre * (1.0 - sigma)))).astype(jnp.bfloat16)
    weight_grad = jnp.dot(aggregated_b.T, signal, preferred_element_type=jnp.float32)
    backed = jnp.dot(signal, weight.T, preferred_element_type=jnp.float32)
    pushed = (norm_scale[:, None] * backed).astype(jnp.bfloat16)
    push_tiles = pushed.reshape(STRIPES, STRIPE_TILES, TILE, FEAT)

    def backward_step(totals, flat_index):
        stripe_id, row_list, col_list, mask_tiles, source_ids = tile_setup(flat_index, tile_rows, tile_cols, tile_masks, tile_counts)
        picked = jnp.take(push_tiles[stripe_id], row_list, axis=0).astype(jnp.float32)
        products = jnp.einsum("kcij,kcif->kcjf", mask_tiles, picked)
        onehot = (col_list[..., None] == tile_ids).astype(jnp.float32)
        partial_sum = jnp.einsum("kcr,kcjf->krjf", onehot, products)
        return totals.at[source_ids].add(partial_sum), None

    returned = lax.scan(backward_step, empty, flat_ids)[0]
    feature_grad = norm_scale[:, None] * returned.reshape(NODES, FEAT)
    return activations, feature_grad, weight_grad
```

```python
import functools

import jax
import jax.numpy as jnp
from jax import lax
from jax.experimental import pallas as pl
from jax.experimental.pallas import tpu as pltpu
from jax.sharding import PartitionSpec as P

TILE = 128
SECTIONS = 16
CAP = 48
STRIPE = 1024
PIECE = 256
FEAT = 128
RING = 8
UNROLL = 4
MESH = pl.DeviceIdType.MESH


def dense_kernel(rows, cols, counts, words, out, packed):
    section = pl.program_id(0)
    live_count = counts[section]
    out[...] = jnp.zeros_like(out)
    for eight in range(CAP // 8):
        slots = pl.ds(eight * 8, 8)
        for part in range(4):
            value = words[0, slots, pl.ds(part * 512, 128)]
            for step in range(1, 4):
                value = value | (words[0, slots, pl.ds(part * 512 + step * 128, 128)] << (8 * step))
            packed[slots, part, :] = value
    lane = lax.broadcasted_iota(jnp.int32, (8, 128), 1)
    row = lax.broadcasted_iota(jnp.int32, (8, 128), 0)
    place = row * 16 + lax.rem(lane, 16)
    bit = lax.div(lane, 16)

    def tile_of(slot):
        live = jnp.where(slot < live_count, 1, 0)
        strips = []
        for part in range(4):
            spread = jnp.broadcast_to(packed[slot, pl.ds(part, 1), :], (8, 128))
            near = jnp.take_along_axis(spread, place, axis=1, mode="promise_in_bounds")
            for step in range(4):
                strips.append(((near >> (bit + 8 * step)) & live).astype(jnp.float32))
        return jnp.concatenate(strips, axis=0).astype(jnp.bfloat16)

    def group_step(group, carry):
        tiles = [tile_of(group * UNROLL + index) for index in range(UNROLL)]
        for index in range(UNROLL):
            slot = group * UNROLL + index
            top = pl.multiple_of(rows[section, slot] * TILE, TILE)
            left = pl.multiple_of(cols[section, slot] * TILE, TILE)
            out[0, pl.ds(top, TILE), pl.ds(left, TILE)] += tiles[index]
        return carry

    lax.fori_loop(0, (live_count + UNROLL - 1) // UNROLL, group_step, 0)


def dense_blocks(tile_rows, tile_cols, tile_counts, tile_masks):
    return pl.pallas_call(
        dense_kernel,
        out_shape=jax.ShapeDtypeStruct((SECTIONS, STRIPE, STRIPE), jnp.bfloat16),
        grid_spec=pltpu.PrefetchScalarGridSpec(
            num_scalar_prefetch=3,
            grid=(SECTIONS,),
            in_specs=[pl.BlockSpec((1, CAP, 2048), lambda k, *_: (k, 0, 0))],
            out_specs=pl.BlockSpec((1, STRIPE, STRIPE), lambda k, *_: (k, 0, 0)),
            scratch_shapes=[pltpu.VMEM((CAP, 4, 128), jnp.int32)],
        ),
        compiler_params=pltpu.CompilerParams(vmem_limit_bytes=32 * 1024 * 1024),
        cost_estimate=pl.CostEstimate(flops=50_000_000, bytes_accessed=40_000_000, transcendentals=0),
    )(tile_rows, tile_cols, tile_counts, tile_masks)


def layer_kernel(
    features, norm, weight, cotangent, dense, act, feature_grad, weight_grad,
    blocks, stripes, own, totals, parts, pushed, own_pushed, sums, going, coming, coming_low, shares, shared, terms, other_terms,
    dense_sem, team_send, team_recv, ring_send, ring_send_low, ring_recv, part_send, part_recv, push_send, push_recv,
    back_send, back_recv, back_recv_low, share_send, share_recv, term_send, term_recv,
):
    loop = lax.axis_index("loop")
    depth = lax.axis_index("depth")
    z = loop // 8
    half = (loop // 4) % 2
    y = loop % 4
    node = loop // 4
    kind = (y - depth + 4) % 4
    first = depth == 0

    def remote(source, target, send, recv, device):
        return pltpu.make_async_remote_copy(
            src_ref=source, dst_ref=target, send_sem=send, recv_sem=recv, device_id=device, device_id_type=MESH
        )

    def toggled(value, bit):
        return value + bit - 2 * bit * ((value // bit) % 2)

    above = (((z + 1) % RING) * 8 + loop % 8, depth)
    below = (((z + RING - 1) % RING) * 8 + loop % 8, depth)
    team = [[((z * 2 + other) * 4 + (y + member) % 4, member) for member in range(4)] for other in range(2)]
    owners = [[((z * 2 + other) * 4 + kind, piece) for piece in range(4)] for other in range(2)]
    beside = [(loop, (depth + offset) % 4) for offset in range(1, 4)]
    before = [(depth + 4 - offset) % 4 for offset in range(1, 4)]
    partners = [
        (loop, toggled(depth, 1)), (loop, toggled(depth, 2)), (toggled(loop, 4), depth), (toggled(loop, 1), depth),
        (toggled(loop, 2), depth), (toggled(loop, 8), depth), (toggled(loop, 16), depth), (toggled(loop, 32), depth),
    ]

    def section_of(slot):
        return ((loop - depth - kind - 4 * slot + 128) // 4) % SECTIONS

    def step_of(index):
        distance = (index + 2) // 4
        up = ((index + 2) // 2) % 2
        other = index % 2
        slot = ((z + RING - distance + 2 * distance * up) % RING) * 2 + other
        passes = (index >= 2) & ((distance < 3) | ((distance == 3) & (other == up)))
        return distance, up, other, slot, passes

    def load_of(section):
        return pltpu.make_async_copy(dense.at[section], blocks.at[section], dense_sem.at[section])

    def load_step(index, carry):
        load_of(section_of(step_of(index)[3])).start()
        return carry

    lax.fori_loop(0, SECTIONS, load_step, 0)

    barrier = pltpu.get_barrier_semaphore()
    for device in [above, below] + beside + [partners[2], partners[3], partners[4], partners[6], partners[7]]:
        pl.semaphore_signal(barrier, inc=1, device_id=device, device_id_type=MESH)
    for other in range(2):
        for index in range(4):
            def greet(other=other, index=index):
                pl.semaphore_signal(barrier, inc=1, device_id=team[other][index], device_id_type=MESH)
                pl.semaphore_signal(barrier, inc=1, device_id=owners[other][index], device_id_type=MESH)

            if index == 0:
                pl.when(jnp.logical_not(first & (half == other)))(greet)
            else:
                greet()

    order_row = lax.broadcasted_iota(jnp.int32, (TILE, TILE), 0)
    order_col = lax.broadcasted_iota(jnp.int32, (TILE, TILE), 1)
    order = jnp.where(order_col == 8 * (order_row % 16) + order_row // 16, 1.0, 0.0)
    norm_row = norm[...]
    norm_full = jnp.broadcast_to(norm_row, (FEAT, PIECE)).T
    scaled = (norm_full * features[...]).astype(jnp.bfloat16)
    for tile in range(2):
        own[pl.ds(tile * TILE, TILE), :] = jnp.dot(
            order.astype(jnp.bfloat16), scaled[tile * TILE:(tile + 1) * TILE], preferred_element_type=jnp.float32
        ).astype(jnp.bfloat16)

    pl.semaphore_wait(barrier, jnp.where(first, 24, 26))

    mine = pl.ds(pl.multiple_of(depth * PIECE, PIECE), PIECE)

    def team_copy(other, member):
        return remote(
            own, stripes.at[node, mine], team_send.at[other, member], team_recv.at[half, depth], team[other][member]
        )

    for other in range(2):
        for member in range(4):
            if member == 0:
                @pl.when(jnp.logical_not(first & (half == other)))
                def _(other=other):
                    team_copy(other, 0).start()
            else:
                team_copy(other, member).start()

    @pl.when(first)
    def _():
        stripes[node, 0:PIECE, :] = own[...]

    totals[...] = jnp.zeros_like(totals)

    def ring_up(slot):
        return remote(stripes.at[slot], stripes.at[slot], ring_send.at[slot], ring_recv.at[slot], above)

    def ring_down(slot):
        return remote(stripes.at[slot], stripes.at[slot], ring_send.at[slot], ring_recv.at[slot], below)

    def ring_down_own(slot, other):
        return remote(stripes.at[slot], stripes.at[slot], ring_send_low.at[other], ring_recv.at[slot], below)

    def forward_step(index, carry):
        distance, up, other, slot, passes = step_of(index)
        section = section_of(slot)

        @pl.when(index < 2)
        def _():
            for piece in range(4):
                def arrived(piece=piece):
                    remote(
                        own, stripes.at[slot, pl.ds(piece * PIECE, PIECE)], team_send.at[0, 0],
                        team_recv.at[other, piece], above,
                    ).wait_recv()

                if piece == 0:
                    pl.when(jnp.logical_not(first & (half == other)))(arrived)
                else:
                    arrived()
            ring_up(slot).start()
            ring_down_own(slot, other).start()

        @pl.when(index >= 2)
        def _():
            ring_up(slot).wait_recv()

        @pl.when(passes & (up == 0))
        def _():
            ring_up(slot).start()

        @pl.when(passes & (up == 1))
        def _():
            ring_down(slot).start()

        load_of(section).wait()
        totals[...] += jnp.dot(blocks[section], stripes[slot], preferred_element_type=jnp.float32)
        return carry

    lax.fori_loop(0, SECTIONS, forward_step, 0)

    def part_copy(offset):
        target = pl.ds(pl.multiple_of(beside[offset][1] * PIECE, PIECE), PIECE)
        return remote(
            totals.at[target], parts.at[offset], part_send.at[offset], part_recv.at[offset], beside[offset]
        )

    for offset in range(3):
        part_copy(offset).start()
    summed = totals[mine, :]
    for offset in range(3):
        part_copy(offset).wait_recv()
        summed = summed + parts[offset]

    aggregated_b = (norm_full * summed).astype(jnp.bfloat16)
    pre = jnp.dot(aggregated_b, weight[...], preferred_element_type=jnp.float32)
    sigma = jax.nn.sigmoid(pre)
    act[...] = pre * sigma
    signal = (cotangent[...] * (sigma * (1.0 + pre * (1.0 - sigma)))).astype(jnp.bfloat16)
    backed = lax.dot_general(weight[...], signal, (((1,), (1,)), ((), ())), preferred_element_type=jnp.float32)
    own_pushed[...] = (norm_row * backed).astype(jnp.bfloat16)

    def push_copy(offset):
        return remote(
            own_pushed, pushed.at[:, mine], push_send.at[offset], push_recv.at[offset], beside[offset]
        )

    for offset in range(3):
        push_copy(offset).start()
    pushed[:, mine] = own_pushed[...]
    terms[0] = lax.dot_general(aggregated_b, signal, (((0,), (0,)), ((), ())), preferred_element_type=jnp.float32)

    def term_copy(step):
        return remote(terms.at[step], other_terms.at[step], term_send.at[step], term_recv.at[step], partners[step])

    term_copy(0).start()
    for offset in range(3):
        source = pl.ds(pl.multiple_of(before[offset] * PIECE, PIECE), PIECE)
        remote(
            own_pushed, pushed.at[:, source], push_send.at[offset], push_recv.at[offset], beside[offset]
        ).wait_recv()

    def share_copy(other, piece):
        return remote(
            shares.at[other, piece], shared.at[half, depth], share_send.at[other, piece], share_recv.at[half, depth],
            owners[other][piece],
        )

    def back_arrived(slot):
        return remote(going.at[slot], coming.at[slot], back_send.at[slot], back_recv.at[slot], above)

    def back_arrived_low(slot, other):
        return remote(going.at[slot], coming_low.at[other], back_send.at[slot], back_recv_low.at[other], below)

    def backward_step(count, carry):
        index = SECTIONS - 1 - count
        distance, up, other, slot, passes = step_of(index)
        section = section_of(slot)
        sums[...] = jnp.dot(pushed[...], blocks[section], preferred_element_type=jnp.float32)

        @pl.when(passes | (index < 2))
        def _():
            back_arrived(slot).wait_recv()
            sums[...] += coming[slot].astype(jnp.float32)

        @pl.when(index < 2)
        def _():
            back_arrived_low(slot, other).wait_recv()
            sums[...] += coming_low[other].astype(jnp.float32)
            for piece in range(4):
                shares[other, piece] = sums[:, piece * PIECE:(piece + 1) * PIECE].astype(jnp.bfloat16)

        for which in range(2):
            @pl.when((index < 2) & (other == which))
            def _(which=which):
                for piece in range(4):
                    if piece == 0:
                        @pl.when(jnp.logical_not(first & (half == which)))
                        def _():
                            share_copy(which, 0).start()

                        @pl.when(first & (half == which))
                        def _():
                            shared[half, 0] = shares[which, 0]
                    else:
                        share_copy(which, piece).start()

        @pl.when(index >= 2)
        def _():
            going[slot] = sums[...].astype(jnp.bfloat16)

        last_far = distance == 4

        @pl.when((index >= 2) & (((up == 0) & jnp.logical_not(last_far)) | (last_far & (other == 0))))
        def _():
            remote(going.at[slot], coming.at[slot], back_send.at[slot], back_recv.at[slot], below).start()

        @pl.when((index >= 2) & (((up == 1) & (distance > 1)) | (last_far & (other == 1))))
        def _():
            remote(going.at[slot], coming.at[slot], back_send.at[slot], back_recv.at[slot], above).start()

        @pl.when((index >= 2) & (up == 1) & (distance == 1))
        def _():
            remote(going.at[slot], coming_low.at[other], back_send.at[slot], back_recv_low.at[other], above).start()

        for step in range(1, 8):
            @pl.when(count == 2 * step)
            def _(step=step):
                term_copy(step - 1).wait_recv()
                terms[step] = terms[step - 1] + other_terms[step - 1]
                term_copy(step).start()

        return carry

    lax.fori_loop(0, SECTIONS, backward_step, 0)

    term_copy(7).wait_recv()
    weight_grad[...] = terms[7] + other_terms[7]

    gathered = jnp.zeros((FEAT, PIECE), jnp.float32)
    for other in range(2):
        for member in range(4):
            def share_arrived(other=other, member=member):
                remote(
                    shares.at[0, 0], shared.at[other, member], share_send.at[0, 0], share_recv.at[other, member], above
                ).wait_recv()

            if member == 0:
                pl.when(jnp.logical_not(first & (half == other)))(share_arrived)
            else:
                share_arrived()
            gathered = gathered + shared[other, member].astype(jnp.float32)
    for tile in range(2):
        feature_grad[pl.ds(tile * TILE, TILE), :] = norm_full[tile * TILE:(tile + 1) * TILE] * lax.dot_general(
            order, gathered[:, tile * TILE:(tile + 1) * TILE], (((0,), (1,)), ((), ())),
            precision=lax.Precision.HIGHEST, preferred_element_type=jnp.float32,
        )

    for other in range(2):
        for index in range(4):
            def sent(other=other, index=index):
                team_copy(other, index).wait_send()
                share_copy(other, index).wait_send()

            if index == 0:
                pl.when(jnp.logical_not(first & (half == other)))(sent)
            else:
                sent()
    for offset in range(3):
        part_copy(offset).wait_send()
        push_copy(offset).wait_send()
    for step in range(8):
        term_copy(step).wait_send()

    def sent_step(index, carry):
        distance, up, other, slot, passes = step_of(index)

        @pl.when(index < 2)
        def _():
            ring_down_own(slot, other).wait_send()

        @pl.when(passes | (index < 2))
        def _():
            ring_up(slot).wait_send()

        @pl.when(index >= 2)
        def _():
            back_arrived(slot).wait_send()

        return carry

    lax.fori_loop(0, SECTIONS, sent_step, 0)


def layer(features, norm_row, weight, cotangent, dense):
    vmem = pl.BlockSpec(memory_space=pltpu.VMEM)
    dma = pltpu.SemaphoreType.DMA
    bf16, f32 = jnp.bfloat16, jnp.float32
    return pl.pallas_call(
        layer_kernel,
        out_shape=(
            jax.ShapeDtypeStruct((PIECE, FEAT), f32),
            jax.ShapeDtypeStruct((PIECE, FEAT), f32),
            jax.ShapeDtypeStruct((FEAT, FEAT), f32),
        ),
        in_specs=[vmem, vmem, vmem, vmem, pl.BlockSpec(memory_space=pl.ANY)],
        out_specs=(vmem, vmem, vmem),
        scratch_shapes=[
            pltpu.VMEM((SECTIONS, STRIPE, STRIPE), bf16),
            pltpu.VMEM((SECTIONS, STRIPE, FEAT), bf16),
            pltpu.VMEM((PIECE, FEAT), bf16),
            pltpu.VMEM((STRIPE, FEAT), f32),
            pltpu.VMEM((3, PIECE, FEAT), f32),
            pltpu.VMEM((FEAT, STRIPE), bf16),
            pltpu.VMEM((FEAT, PIECE), bf16),
            pltpu.VMEM((FEAT, STRIPE), f32),
            pltpu.VMEM((SECTIONS, FEAT, STRIPE), bf16),
            pltpu.VMEM((SECTIONS, FEAT, STRIPE), bf16),
            pltpu.VMEM((2, FEAT, STRIPE), bf16),
            pltpu.VMEM((2, 4, FEAT, PIECE), bf16),
            pltpu.VMEM((2, 4, FEAT, PIECE), bf16),
            pltpu.VMEM((8, FEAT, FEAT), f32),
            pltpu.VMEM((8, FEAT, FEAT), f32),
            dma((SECTIONS,)), dma((2, 4)), dma((2, 4)), dma((SECTIONS,)), dma((2,)), dma((SECTIONS,)),
            dma((3,)), dma((3,)), dma((3,)), dma((3,)),
            dma((SECTIONS,)), dma((SECTIONS,)), dma((2,)), dma((2, 4)), dma((2, 4)), dma((8,)), dma((8,)),
        ],
        compiler_params=pltpu.CompilerParams(
            collective_id=0, has_side_effects=True, vmem_limit_bytes=60 * 1024 * 1024
        ),
        cost_estimate=pl.CostEstimate(flops=9_000_000_000, bytes_accessed=34_000_000, transcendentals=32768),
    )(features, norm_row, weight, cotangent, dense)


def per_device(features, norm_scale, weight, cotangent, tile_rows, tile_cols, tile_masks, tile_counts):
    dense = dense_blocks(tile_rows[0, 0], tile_cols[0, 0], tile_counts[0, 0], tile_masks[0, 0])
    return layer(features, norm_scale.reshape(1, -1), weight, cotangent, dense)


def solution(mesh):
    return jax.shard_map(
        per_device,
        mesh=mesh,
        in_specs=(
            P(("loop", "depth"), None),
            P(("loop", "depth")),
            P(),
            P(("loop", "depth"), None),
            P("loop", "depth", None, None),
            P("loop", "depth", None, None),
            P("loop", "depth", None, None, None),
            P("loop", "depth", None),
        ),
        out_specs=(P(("loop", "depth"), None), P(("loop", "depth"), None), P()),
        check_vma=False,
    )
```

```python
import jax
import jax.numpy as jnp
from jax import lax
from jax.experimental import pallas as pl
from jax.experimental.pallas import tpu as pltpu
from jax.sharding import PartitionSpec as P

TILE = 128
SECTIONS = 16
CAP = 48
STRIPE = 1024
PIECE = 256
FEAT = 128
RING = 8
UNROLL = 4
WIDE = 512
LAG = 2
MESH = pl.DeviceIdType.MESH


def dense_kernel(rows, cols, counts, words, out, packed):
    section = pl.program_id(0)
    live_count = counts[section]
    out[...] = jnp.zeros_like(out)
    packed[pl.ds(CAP, UNROLL)] = jnp.zeros((UNROLL, 4, 128), jnp.int32)
    for eight in range(CAP // 8):
        slots = pl.ds(eight * 8, 8)
        for part in range(4):
            value = words[0, slots, pl.ds(part * 512, 128)]
            for step in range(1, 4):
                value = value | (words[0, slots, pl.ds(part * 512 + step * 128, 128)] << (8 * step))
            packed[slots, part, :] = value
    lane = lax.broadcasted_iota(jnp.int32, (8, 128), 1)
    row = lax.broadcasted_iota(jnp.int32, (8, 128), 0)
    place = row * 16 + lax.rem(lane, 16)
    bit = lax.div(lane, 16)

    def near_of(group):
        return [
            jnp.take_along_axis(
                jnp.broadcast_to(packed[group * UNROLL + index, pl.ds(part, 1), :], (8, 128)),
                place, axis=1, mode="promise_in_bounds",
            )
            for index in range(UNROLL) for part in range(4)
        ]

    def group_step(group, nears):
        later = near_of(group + 1)
        for index in range(UNROLL):
            slot = group * UNROLL + index
            live = jnp.where(slot < live_count, 1, 0)
            strips = [
                ((nears[4 * index + part] >> (bit + 8 * step)) & live).astype(jnp.float32)
                for part in range(4) for step in range(4)
            ]
            tile = jnp.concatenate(strips, axis=0).astype(jnp.bfloat16)
            top = pl.multiple_of(rows[section, slot] * TILE, TILE)
            left = pl.multiple_of(cols[section, slot] * TILE, TILE)
            out[0, pl.ds(top, TILE), pl.ds(left, TILE)] += tile
        return later

    lax.fori_loop(0, (live_count + UNROLL - 1) // UNROLL, group_step, near_of(0))


def dense_blocks(tile_rows, tile_cols, tile_counts, tile_masks):
    return pl.pallas_call(
        dense_kernel,
        out_shape=jax.ShapeDtypeStruct((SECTIONS, STRIPE, STRIPE), jnp.bfloat16),
        grid_spec=pltpu.PrefetchScalarGridSpec(
            num_scalar_prefetch=3,
            grid=(SECTIONS,),
            in_specs=[pl.BlockSpec((1, CAP, 2048), lambda k, *_: (k, 0, 0))],
            out_specs=pl.BlockSpec((1, STRIPE, STRIPE), lambda k, *_: (k, 0, 0)),
            scratch_shapes=[pltpu.VMEM((CAP + UNROLL, 4, 128), jnp.int32)],
        ),
        compiler_params=pltpu.CompilerParams(vmem_limit_bytes=60 * 1024 * 1024),
        cost_estimate=pl.CostEstimate(flops=50_000_000, bytes_accessed=40_000_000, transcendentals=0),
    )(tile_rows, tile_cols, tile_counts, tile_masks)


def layer_kernel(
    features, norm, weight, cotangent, dense, act, feature_grad, weight_grad,
    blocks, stripes, own, totals, parts, pushed, own_pushed, sums, going, going_thin, coming, coming_thin, coming_low,
    coming_thin_low, given, taken, shares, shared, terms, other_terms,
    dense_sem, team_send, team_recv, ring_send, ring_send_low, ring_recv, thin_send, thin_send_low, thin_recv, peer_send,
    peer_recv, part_send, part_recv, push_send, push_recv, back_send, back_recv, back_recv_low, back_thin_send,
    back_thin_recv, back_thin_recv_low, give_send, give_recv, share_send, share_recv, term_send, term_recv,
):
    loop = lax.axis_index("loop")
    depth = lax.axis_index("depth")
    z = loop // 8
    half = (loop // 4) % 2
    y = loop % 4
    node = loop // 4
    kind = (y - depth + 4) % 4
    first = depth == 0

    def remote(source, target, send, recv, device):
        return pltpu.make_async_remote_copy(
            src_ref=source, dst_ref=target, send_sem=send, recv_sem=recv, device_id=device, device_id_type=MESH
        )

    def toggled(value, bit):
        return value + bit - 2 * bit * ((value // bit) % 2)

    above = (((z + 1) % RING) * 8 + loop % 8, depth)
    below = (((z + RING - 1) % RING) * 8 + loop % 8, depth)
    team = [[((z * 2 + other) * 4 + (y + member) % 4, member) for member in range(4)] for other in range(2)]
    owners = [[((z * 2 + other) * 4 + kind, piece) for piece in range(4)] for other in range(2)]
    beside = [(loop, (depth + offset) % 4) for offset in range(1, 4)]
    peers = [(depth + offset) % 4 for offset in range(1, 4)]
    peer_devices = [(node * 4 + (kind + member) % 4, member) for member in peers]
    before = [(depth + 4 - offset) % 4 for offset in range(1, 4)]
    partners = [
        (loop, toggled(depth, 1)), (loop, toggled(depth, 2)), (toggled(loop, 4), depth), (toggled(loop, 1), depth),
        (toggled(loop, 2), depth), (toggled(loop, 8), depth), (toggled(loop, 16), depth), (toggled(loop, 32), depth),
    ]

    def section_of(slot):
        return ((loop - depth - kind - 4 * slot + 128) // 4) % SECTIONS

    def step_of(index):
        distance = (index + 2) // 4
        up = ((index + 2) // 2) % 2
        other = index % 2
        slot = ((z + RING - distance + 2 * distance * up) % RING) * 2 + other
        passes = (index >= 2) & ((distance < 3) | ((distance == 3) & (other == up)))
        return distance, up, other, slot, passes

    def load_of(section):
        return pltpu.make_async_copy(dense.at[section], blocks.at[section], dense_sem.at[section])

    def load_step(index, carry):
        load_of(section_of(step_of(index)[3])).start()
        return carry

    lax.fori_loop(0, SECTIONS, load_step, 0)

    barrier = pltpu.get_barrier_semaphore()
    for device in [above, below] + beside + peer_devices + [partners[2], partners[3], partners[4], partners[6], partners[7]]:
        pl.semaphore_signal(barrier, inc=1, device_id=device, device_id_type=MESH)
    for other in range(2):
        for index in range(4):
            def greet(other=other, index=index):
                pl.semaphore_signal(barrier, inc=1, device_id=team[other][index], device_id_type=MESH)
                pl.semaphore_signal(barrier, inc=1, device_id=owners[other][index], device_id_type=MESH)

            if index == 0:
                pl.when(jnp.logical_not(first & (half == other)))(greet)
            else:
                greet()

    order_row = lax.broadcasted_iota(jnp.int32, (TILE, TILE), 0)
    order_col = lax.broadcasted_iota(jnp.int32, (TILE, TILE), 1)
    order = jnp.where(order_col == 8 * (order_row % 16) + order_row // 16, 1.0, 0.0)
    norm_row = norm[...]
    norm_full = jnp.broadcast_to(norm_row, (FEAT, PIECE)).T
    scaled = (norm_full * features[...]).astype(jnp.bfloat16)
    for tile in range(2):
        own[pl.ds(tile * TILE, TILE), :] = jnp.dot(
            order.astype(jnp.bfloat16), scaled[tile * TILE:(tile + 1) * TILE], preferred_element_type=jnp.float32
        ).astype(jnp.bfloat16)

    pl.semaphore_wait(barrier, jnp.where(first, 27, 29))

    mine = pl.ds(pl.multiple_of(depth * PIECE, PIECE), PIECE)

    def team_copy(other, member):
        return remote(
            own, stripes.at[node, mine], team_send.at[other, member], team_recv.at[half, depth], team[other][member]
        )

    for other in range(2):
        for member in range(4):
            if member == 0:
                @pl.when(jnp.logical_not(first & (half == other)))
                def _(other=other):
                    team_copy(other, 0).start()
            else:
                team_copy(other, member).start()

    @pl.when(first)
    def _():
        stripes[node, 0:PIECE, :] = own[...]

    totals[...] = jnp.zeros_like(totals)

    wide = pl.ds(0, WIDE)
    thin = pl.ds(pl.multiple_of(WIDE + TILE * depth, TILE), TILE)

    def ring_copy(slot, send, device):
        rows = stripes.at[slot, wide]
        return remote(rows, rows, send, ring_recv.at[slot], device)

    def thin_copy(slot, send, device):
        rows = stripes.at[slot, thin]
        return remote(rows, rows, send, thin_recv.at[slot], device)

    def peer_copy(slot, offset):
        rows = stripes.at[slot, thin]
        return remote(rows, rows, peer_send.at[slot, offset], peer_recv.at[slot, depth], peer_devices[offset])

    def peer_arrived(slot, offset):
        rows = stripes.at[slot, pl.ds(pl.multiple_of(WIDE + TILE * peers[offset], TILE), TILE)]
        return remote(
            rows, rows, peer_send.at[slot, offset], peer_recv.at[slot, peers[offset]], peer_devices[offset]
        )

    def pass_on(index):
        distance, up, other, slot, passes = step_of(index)

        @pl.when(index < 2)
        def _():
            for piece in range(4):
                def arrived(piece=piece):
                    remote(
                        own, stripes.at[slot, pl.ds(piece * PIECE, PIECE)], team_send.at[0, 0],
                        team_recv.at[other, piece], above,
                    ).wait_recv()

                if piece == 0:
                    pl.when(jnp.logical_not(first & (half == other)))(arrived)
                else:
                    arrived()
            thin_copy(slot, thin_send.at[slot], above).start()
            thin_copy(slot, thin_send_low.at[other], below).start()
            ring_copy(slot, ring_send.at[slot], above).start()
            ring_copy(slot, ring_send_low.at[other], below).start()

        @pl.when(index >= 2)
        def _():
            thin_copy(slot, thin_send.at[slot], above).wait_recv()

        @pl.when(passes & (up == 0))
        def _():
            thin_copy(slot, thin_send.at[slot], above).start()

        @pl.when(passes & (up == 1))
        def _():
            thin_copy(slot, thin_send.at[slot], below).start()

        @pl.when(index >= 2)
        def _():
            for offset in range(3):
                peer_copy(slot, offset).start()
            ring_copy(slot, ring_send.at[slot], above).wait_recv()

        @pl.when(passes & (up == 0))
        def _():
            ring_copy(slot, ring_send.at[slot], above).start()

        @pl.when(passes & (up == 1))
        def _():
            ring_copy(slot, ring_send.at[slot], below).start()

    def forward_step(count, carry):
        @pl.when(count < SECTIONS)
        def _():
            pass_on(count)

        @pl.when(count >= LAG)
        def _():
            index = count - LAG
            slot = step_of(index)[3]
            section = section_of(slot)

            @pl.when(index >= 2)
            def _():
                for offset in range(3):
                    peer_arrived(slot, offset).wait_recv()

            load_of(section).wait()
            totals[...] += jnp.dot(blocks[section], stripes[slot], preferred_element_type=jnp.float32)

        return carry

    lax.fori_loop(0, SECTIONS + LAG, forward_step, 0)

    def part_copy(offset):
        target = pl.ds(pl.multiple_of(beside[offset][1] * PIECE, PIECE), PIECE)
        return remote(
            totals.at[target], parts.at[offset], part_send.at[offset], part_recv.at[offset], beside[offset]
        )

    for offset in range(3):
        part_copy(offset).start()
    summed = totals[mine, :]
    for offset in range(3):
        part_copy(offset).wait_recv()
        summed = summed + parts[offset]

    aggregated_b = (norm_full * summed).astype(jnp.bfloat16)
    pre = jnp.dot(aggregated_b, weight[...], preferred_element_type=jnp.float32)
    sigma = jax.nn.sigmoid(pre)
    act[...] = pre * sigma
    signal = (cotangent[...] * (sigma * (1.0 + pre * (1.0 - sigma)))).astype(jnp.bfloat16)
    backed = lax.dot_general(weight[...], signal, (((1,), (1,)), ((), ())), preferred_element_type=jnp.float32)
    own_pushed[...] = (norm_row * backed).astype(jnp.bfloat16)

    def push_copy(offset):
        return remote(
            own_pushed, pushed.at[:, mine], push_send.at[offset], push_recv.at[offset], beside[offset]
        )

    for offset in range(3):
        push_copy(offset).start()
    pushed[:, mine] = own_pushed[...]
    terms[0] = lax.dot_general(aggregated_b, signal, (((0,), (0,)), ((), ())), preferred_element_type=jnp.float32)

    def term_copy(step):
        return remote(terms.at[step], other_terms.at[step], term_send.at[step], term_recv.at[step], partners[step])

    term_copy(0).start()
    for offset in range(3):
        source = pl.ds(pl.multiple_of(before[offset] * PIECE, PIECE), PIECE)
        remote(
            own_pushed, pushed.at[:, source], push_send.at[offset], push_recv.at[offset], beside[offset]
        ).wait_recv()

    def share_copy(other, piece):
        return remote(
            shares.at[other, piece], shared.at[half, depth], share_send.at[other, piece], share_recv.at[half, depth],
            owners[other][piece],
        )

    def back_copy(slot, target, recv, device):
        return remote(going.at[slot], target, back_send.at[slot], recv, device)

    def back_thin_copy(slot, target, recv, device):
        return remote(going_thin.at[slot], target, back_thin_send.at[slot], recv, device)

    def give_copy(slot, offset):
        return remote(
            given.at[slot, offset], taken.at[slot, depth], give_send.at[slot, offset], give_recv.at[slot, depth],
            peer_devices[offset],
        )

    def give_arrived(slot, offset):
        return remote(
            given.at[slot, offset], taken.at[slot, peers[offset]], give_send.at[slot, offset],
            give_recv.at[slot, peers[offset]], peer_devices[offset],
        )

    def multiply(index, held):
        slot = step_of(index)[3]
        sums[held] = jnp.dot(pushed[...], blocks[section_of(slot)], preferred_element_type=jnp.float32)

        @pl.when(index >= 2)
        def _():
            for offset in range(3):
                lanes = pl.ds(pl.multiple_of(WIDE + TILE * peers[offset], TILE), TILE)
                given[slot, offset] = sums[held, :, lanes].astype(jnp.bfloat16)
                give_copy(slot, offset).start()

    def reduce(index, held):
        distance, up, other, slot, passes = step_of(index)

        @pl.when(index >= 2)
        def _():
            for offset in range(3):
                give_arrived(slot, offset).wait_recv()
                sums[held, :, thin] += taken[slot, peers[offset]].astype(jnp.float32)

        @pl.when(passes | (index < 2))
        def _():
            back_thin_copy(slot, coming_thin.at[slot], back_thin_recv.at[slot], above).wait_recv()
            sums[held, :, thin] += coming_thin[slot].astype(jnp.float32)
            back_copy(slot, coming.at[slot], back_recv.at[slot], above).wait_recv()
            sums[held, :, wide] += coming[slot].astype(jnp.float32)

        @pl.when(index < 2)
        def _():
            back_thin_copy(slot, coming_thin_low.at[other], back_thin_recv_low.at[other], below).wait_recv()
            sums[held, :, thin] += coming_thin_low[other].astype(jnp.float32)
            back_copy(slot, coming_low.at[other], back_recv_low.at[other], below).wait_recv()
            sums[held, :, wide] += coming_low[other].astype(jnp.float32)
            for piece in range(4):
                shares[other, piece] = sums[held, :, pl.ds(piece * PIECE, PIECE)].astype(jnp.bfloat16)

        for which in range(2):
            @pl.when((index < 2) & (other == which))
            def _(which=which):
                for piece in range(4):
                    if piece == 0:
                        @pl.when(jnp.logical_not(first & (half == which)))
                        def _():
                            share_copy(which, 0).start()

                        @pl.when(first & (half == which))
                        def _():
                            shared[half, 0] = shares[which, 0]
                    else:
                        share_copy(which, piece).start()

        @pl.when(index >= 2)
        def _():
            going_thin[slot] = sums[held, :, thin].astype(jnp.bfloat16)
            going[slot] = sums[held, :, wide].astype(jnp.bfloat16)

        last_far = distance == 4

        @pl.when((index >= 2) & (((up == 0) & jnp.logical_not(last_far)) | (last_far & (other == 0))))
        def _():
            back_thin_copy(slot, coming_thin.at[slot], back_thin_recv.at[slot], below).start()
            back_copy(slot, coming.at[slot], back_recv.at[slot], below).start()

        @pl.when((index >= 2) & (((up == 1) & (distance > 1)) | (last_far & (other == 1))))
        def _():
            back_thin_copy(slot, coming_thin.at[slot], back_thin_recv.at[slot], above).start()
            back_copy(slot, coming.at[slot], back_recv.at[slot], above).start()

        @pl.when((index >= 2) & (up == 1) & (distance == 1))
        def _():
            back_thin_copy(slot, coming_thin_low.at[other], back_thin_recv_low.at[other], above).start()
            back_copy(slot, coming_low.at[other], back_recv_low.at[other], above).start()

    def backward_step(count, carry):
        @pl.when(count < SECTIONS)
        def _():
            multiply(SECTIONS - 1 - count, count % (LAG + 1))

        @pl.when(count >= LAG)
        def _():
            reduce(SECTIONS - 1 - (count - LAG), (count - LAG) % (LAG + 1))

        for step in range(1, 8):
            @pl.when(count == 2 * step)
            def _(step=step):
                term_copy(step - 1).wait_recv()
                terms[step] = terms[step - 1] + other_terms[step - 1]
                term_copy(step).start()

        return carry

    lax.fori_loop(0, SECTIONS + LAG, backward_step, 0)

    term_copy(7).wait_recv()
    weight_grad[...] = terms[7] + other_terms[7]

    gathered = jnp.zeros((FEAT, PIECE), jnp.float32)
    for other in range(2):
        for member in range(4):
            def share_arrived(other=other, member=member):
                remote(
                    shares.at[0, 0], shared.at[other, member], share_send.at[0, 0], share_recv.at[other, member], above
                ).wait_recv()

            if member == 0:
                pl.when(jnp.logical_not(first & (half == other)))(share_arrived)
            else:
                share_arrived()
            gathered = gathered + shared[other, member].astype(jnp.float32)
    for tile in range(2):
        feature_grad[pl.ds(tile * TILE, TILE), :] = norm_full[tile * TILE:(tile + 1) * TILE] * lax.dot_general(
            order, gathered[:, tile * TILE:(tile + 1) * TILE], (((0,), (1,)), ((), ())),
            precision=lax.Precision.HIGHEST, preferred_element_type=jnp.float32,
        )

    for other in range(2):
        for index in range(4):
            def sent(other=other, index=index):
                team_copy(other, index).wait_send()
                share_copy(other, index).wait_send()

            if index == 0:
                pl.when(jnp.logical_not(first & (half == other)))(sent)
            else:
                sent()
    for offset in range(3):
        part_copy(offset).wait_send()
        push_copy(offset).wait_send()
    for step in range(8):
        term_copy(step).wait_send()

    def sent_step(index, carry):
        distance, up, other, slot, passes = step_of(index)

        @pl.when(index < 2)
        def _():
            ring_copy(slot, ring_send_low.at[other], below).wait_send()
            thin_copy(slot, thin_send_low.at[other], below).wait_send()

        @pl.when(passes | (index < 2))
        def _():
            ring_copy(slot, ring_send.at[slot], above).wait_send()
            thin_copy(slot, thin_send.at[slot], above).wait_send()

        @pl.when(index >= 2)
        def _():
            back_copy(slot, coming.at[slot], back_recv.at[slot], above).wait_send()
            back_thin_copy(slot, coming_thin.at[slot], back_thin_recv.at[slot], above).wait_send()
            for offset in range(3):
                peer_copy(slot, offset).wait_send()
                give_copy(slot, offset).wait_send()

        return carry

    lax.fori_loop(0, SECTIONS, sent_step, 0)


def finish_kernel(act, feature_grad, weight_grad, act_out, feature_out, weight_out):
    act_out[...] = act[...]
    feature_out[...] = feature_grad[...]
    weight_out[...] = weight_grad[...]


def finish(*results):
    vmem = pl.BlockSpec(memory_space=pltpu.VMEM)
    return pl.pallas_call(
        finish_kernel,
        out_shape=tuple(jax.ShapeDtypeStruct(value.shape, value.dtype) for value in results),
        in_specs=[vmem] * 3,
        out_specs=(vmem,) * 3,
        cost_estimate=pl.CostEstimate(flops=0, bytes_accessed=640_000, transcendentals=0),
    )(*results)


def layer(features, norm_row, weight, cotangent, dense):
    vmem = pl.BlockSpec(memory_space=pltpu.VMEM)
    dma = pltpu.SemaphoreType.DMA
    bf16, f32 = jnp.bfloat16, jnp.float32
    return pl.pallas_call(
        layer_kernel,
        out_shape=(
            jax.ShapeDtypeStruct((PIECE, FEAT), f32),
            jax.ShapeDtypeStruct((PIECE, FEAT), f32),
            jax.ShapeDtypeStruct((FEAT, FEAT), f32),
        ),
        in_specs=[vmem, vmem, vmem, vmem, pl.BlockSpec(memory_space=pl.ANY)],
        out_specs=(vmem, vmem, vmem),
        scratch_shapes=[
            pltpu.VMEM((SECTIONS, STRIPE, STRIPE), bf16),
            pltpu.VMEM((SECTIONS, STRIPE, FEAT), bf16),
            pltpu.VMEM((PIECE, FEAT), bf16),
            pltpu.VMEM((STRIPE, FEAT), f32),
            pltpu.VMEM((3, PIECE, FEAT), f32),
            pltpu.VMEM((FEAT, STRIPE), bf16),
            pltpu.VMEM((FEAT, PIECE), bf16),
            pltpu.VMEM((LAG + 1, FEAT, STRIPE), f32),
            pltpu.VMEM((SECTIONS, FEAT, WIDE), bf16),
            pltpu.VMEM((SECTIONS, FEAT, TILE), bf16),
            pltpu.VMEM((SECTIONS, FEAT, WIDE), bf16),
            pltpu.VMEM((SECTIONS, FEAT, TILE), bf16),
            pltpu.VMEM((2, FEAT, WIDE), bf16),
            pltpu.VMEM((2, FEAT, TILE), bf16),
            pltpu.VMEM((SECTIONS, 3, FEAT, TILE), bf16),
            pltpu.VMEM((SECTIONS, 4, FEAT, TILE), bf16),
            pltpu.VMEM((2, 4, FEAT, PIECE), bf16),
            pltpu.VMEM((2, 4, FEAT, PIECE), bf16),
            pltpu.VMEM((8, FEAT, FEAT), f32),
            pltpu.VMEM((8, FEAT, FEAT), f32),
            dma((SECTIONS,)), dma((2, 4)), dma((2, 4)), dma((SECTIONS,)), dma((2,)), dma((SECTIONS,)),
            dma((SECTIONS,)), dma((2,)), dma((SECTIONS,)), dma((SECTIONS, 3)), dma((SECTIONS, 4)),
            dma((3,)), dma((3,)), dma((3,)), dma((3,)),
            dma((SECTIONS,)), dma((SECTIONS,)), dma((2,)), dma((SECTIONS,)), dma((SECTIONS,)), dma((2,)),
            dma((SECTIONS, 3)), dma((SECTIONS, 4)),
            dma((2, 4)), dma((2, 4)), dma((8,)), dma((8,)),
        ],
        compiler_params=pltpu.CompilerParams(
            collective_id=0, has_side_effects=True, vmem_limit_bytes=60 * 1024 * 1024
        ),
        cost_estimate=pl.CostEstimate(flops=9_000_000_000, bytes_accessed=34_000_000, transcendentals=32768),
    )(features, norm_row, weight, cotangent, dense)


def per_device(features, norm_scale, weight, cotangent, tile_rows, tile_cols, tile_masks, tile_counts):
    dense = dense_blocks(tile_rows[0, 0], tile_cols[0, 0], tile_counts[0, 0], tile_masks[0, 0])
    return finish(*layer(features, norm_scale.reshape(1, -1), weight, cotangent, dense))


def solution(mesh):
    return jax.shard_map(
        per_device,
        mesh=mesh,
        in_specs=(
            P(("loop", "depth"), None),
            P(("loop", "depth")),
            P(),
            P(("loop", "depth"), None),
            P("loop", "depth", None, None),
            P("loop", "depth", None, None),
            P("loop", "depth", None, None, None),
            P("loop", "depth", None),
        ),
        out_specs=(P(("loop", "depth"), None), P(("loop", "depth"), None), P()),
        check_vma=False,
    )
```

```python
import jax
import jax.numpy as jnp
from jax import lax
from jax.experimental import pallas as pl
from jax.experimental.pallas import tpu as pltpu
from jax.sharding import PartitionSpec as P

TILE = 128
SECTIONS = 16
CAP = 48
STRIPE = 1024
PIECE = 256
FEAT = 128
RING = 8
UNROLL = 4
WIDE = 512
LAG = 3
PAIR = 2
MESH = pl.DeviceIdType.MESH


def dense_kernel(rows, cols, counts, words, out, packed):
    lane = lax.broadcasted_iota(jnp.int32, (8, 128), 1)
    row = lax.broadcasted_iota(jnp.int32, (8, 128), 0)
    place = row * 16 + lax.rem(lane, 16)
    bit = lax.div(lane, 16)
    out[...] = jnp.zeros_like(out)
    for which in range(PAIR):
        packed[which, pl.ds(CAP, UNROLL)] = jnp.zeros((UNROLL, 4, 128), jnp.int32)
        for eight in range(CAP // 8):
            slots = pl.ds(eight * 8, 8)
            for part in range(4):
                value = words[which, slots, pl.ds(part * 512, 128)]
                for step in range(1, 4):
                    value = value | (words[which, slots, pl.ds(part * 512 + step * 128, 128)] << (8 * step))
                packed[which, slots, part, :] = value

    for which in range(PAIR):
        section = pl.program_id(0) * PAIR + which
        live_count = counts[section]

        def near_of(group, which=which):
            return [
                jnp.take_along_axis(
                    jnp.broadcast_to(packed[which, group * UNROLL + index, pl.ds(part, 1), :], (8, 128)),
                    place, axis=1, mode="promise_in_bounds",
                )
                for index in range(UNROLL) for part in range(4)
            ]

        def group_step(group, nears, which=which, section=section, live_count=live_count, near_of=near_of):
            later = near_of(group + 1)
            for index in range(UNROLL):
                slot = group * UNROLL + index
                live = jnp.where(slot < live_count, 1, 0)
                strips = [
                    ((nears[4 * index + part] >> (bit + 8 * step)) & live).astype(jnp.float32)
                    for part in range(4) for step in range(4)
                ]
                tile = jnp.concatenate(strips, axis=0).astype(jnp.bfloat16)
                top = pl.multiple_of(rows[section, slot] * TILE, TILE)
                left = pl.multiple_of(cols[section, slot] * TILE, TILE)
                out[which, pl.ds(top, TILE), pl.ds(left, TILE)] += tile
            return later

        lax.fori_loop(0, (live_count + UNROLL - 1) // UNROLL, group_step, near_of(0))


def dense_blocks(tile_rows, tile_cols, tile_counts, tile_masks):
    return pl.pallas_call(
        dense_kernel,
        out_shape=jax.ShapeDtypeStruct((SECTIONS, STRIPE, STRIPE), jnp.bfloat16),
        grid_spec=pltpu.PrefetchScalarGridSpec(
            num_scalar_prefetch=3,
            grid=(SECTIONS // PAIR,),
            in_specs=[pl.BlockSpec((PAIR, CAP, 2048), lambda k, *_: (k, 0, 0))],
            out_specs=pl.BlockSpec((PAIR, STRIPE, STRIPE), lambda k, *_: (k, 0, 0)),
            scratch_shapes=[pltpu.VMEM((PAIR, CAP + UNROLL, 4, 128), jnp.int32)],
        ),
        compiler_params=pltpu.CompilerParams(vmem_limit_bytes=60 * 1024 * 1024),
        cost_estimate=pl.CostEstimate(flops=50_000_000, bytes_accessed=40_000_000, transcendentals=0),
    )(tile_rows, tile_cols, tile_counts, tile_masks)


def layer_kernel(
    features, norm, weight, cotangent, dense, act, feature_grad, weight_grad,
    blocks, stripes, own, mate, mate_out, mate_in, totals, parting, parts, pushed, own_pushed, sums, going, going_thin, coming, coming_thin, coming_low,
    coming_thin_low, given, taken, shares, shared, terms, other_terms,
    dense_sem, mate_send, mate_recv, mate_back_send, mate_back_recv, team_send, team_recv, ring_send, ring_send_low, ring_recv, thin_send, thin_send_low, thin_recv, peer_send,
    peer_recv, part_send, part_recv, push_send, push_recv, back_send, back_recv, back_recv_low, back_thin_send,
    back_thin_recv, back_thin_recv_low, give_send, give_recv, share_send, share_recv, term_send, term_recv,
):
    loop = lax.axis_index("loop")
    depth = lax.axis_index("depth")
    z = loop // 8
    half = (loop // 4) % 2
    y = loop % 4
    node = loop // 4
    kind = (y - depth + 4) % 4
    first = depth == 0

    def remote(source, target, send, recv, device):
        return pltpu.make_async_remote_copy(
            src_ref=source, dst_ref=target, send_sem=send, recv_sem=recv, device_id=device, device_id_type=MESH
        )

    def toggled(value, bit):
        return value + bit - 2 * bit * ((value // bit) % 2)

    above = (((z + 1) % RING) * 8 + loop % 8, depth)
    below = (((z + RING - 1) % RING) * 8 + loop % 8, depth)
    mate_node = z * 2 + 1 - half
    mate_device = (mate_node * 4 + y, depth)
    team = [(node * 4 + (y + member) % 4, member) for member in range(4)]
    owners = [(node * 4 + kind, piece) for piece in range(4)]
    beside = [(loop, (depth + offset) % 4) for offset in range(1, 4)]
    two = (depth + 2) % 4

    def peer_device(member):
        return (node * 4 + (kind + member) % 4, member)

    def around(other):
        return (depth + 3 + 2 * other) % 4, (depth + 1 + 2 * other) % 4

    before = [(depth + 4 - offset) % 4 for offset in range(1, 4)]
    partners = [
        (loop, toggled(depth, 1)), (loop, toggled(depth, 2)), (toggled(loop, 4), depth), (toggled(loop, 1), depth),
        (toggled(loop, 2), depth), (toggled(loop, 8), depth), (toggled(loop, 16), depth), (toggled(loop, 32), depth),
    ]

    def section_of(slot):
        return ((loop - depth - kind - 4 * slot + 128) // 4) % SECTIONS

    def step_of(index):
        distance = (index + 2) // 4
        up = ((index + 2) // 2) % 2
        other = index % 2
        slot = ((z + RING - distance + 2 * distance * up) % RING) * 2 + (half + other) % 2
        passes = (index >= 2) & ((distance < 3) | ((distance == 3) & (other == up)))
        return distance, up, other, slot, passes

    def load_of(section):
        return pltpu.make_async_copy(dense.at[section], blocks.at[section], dense_sem.at[section])

    def load_step(index, carry):
        load_of(section_of(step_of(index)[3])).start()
        return carry

    lax.fori_loop(0, SECTIONS, load_step, 0)

    barrier = pltpu.get_barrier_semaphore()
    for device in [above, below] + beside + [peer_device((depth + offset) % 4) for offset in range(1, 4)] + [mate_device, partners[3], partners[4], partners[6], partners[7]]:
        pl.semaphore_signal(barrier, inc=1, device_id=device, device_id_type=MESH)
    for index in range(4):
        def greet(index=index):
            pl.semaphore_signal(barrier, inc=1, device_id=team[index], device_id_type=MESH)
            pl.semaphore_signal(barrier, inc=1, device_id=owners[index], device_id_type=MESH)

        if index == 0:
            pl.when(jnp.logical_not(first))(greet)
        else:
            greet()

    order_row = lax.broadcasted_iota(jnp.int32, (TILE, TILE), 0)
    order_col = lax.broadcasted_iota(jnp.int32, (TILE, TILE), 1)
    order = jnp.where(order_col == 8 * (order_row % 16) + order_row // 16, 1.0, 0.0)
    norm_row = norm[...]
    norm_full = jnp.broadcast_to(norm_row, (FEAT, PIECE)).T
    scaled = (norm_full * features[...]).astype(jnp.bfloat16)
    for tile in range(2):
        own[pl.ds(tile * TILE, TILE), :] = jnp.dot(
            order.astype(jnp.bfloat16), scaled[tile * TILE:(tile + 1) * TILE], preferred_element_type=jnp.float32
        ).astype(jnp.bfloat16)

    pl.semaphore_wait(barrier, jnp.where(first, 19, 21))

    mine = pl.ds(pl.multiple_of(depth * PIECE, PIECE), PIECE)

    def team_copy(other, member):
        return remote(
            own if other == 0 else mate, stripes.at[node if other == 0 else mate_node, mine],
            team_send.at[other, member], team_recv.at[other, depth], team[member],
        )

    mate_copy = remote(own, mate, mate_send, mate_recv, mate_device)
    mate_copy.start()
    for other in range(2):
        if other == 1:
            mate_copy.wait_recv()
        for member in range(4):
            if member == 0:
                @pl.when(jnp.logical_not(first))
                def _(other=other):
                    team_copy(other, 0).start()
            else:
                team_copy(other, member).start()

    @pl.when(first)
    def _():
        stripes[node, 0:PIECE, :] = own[...]
        stripes[mate_node, 0:PIECE, :] = mate[...]

    totals[...] = jnp.zeros_like(totals)

    wide = pl.ds(0, WIDE)
    thin = pl.ds(pl.multiple_of(WIDE + TILE * depth, TILE), TILE)

    def ring_copy(slot, send, device):
        rows = stripes.at[slot, wide]
        return remote(rows, rows, send, ring_recv.at[slot], device)

    def thin_copy(slot, send, device):
        rows = stripes.at[slot, thin]
        return remote(rows, rows, send, thin_recv.at[slot], device)

    def quarter(slot, member):
        return stripes.at[slot, pl.ds(pl.multiple_of(WIDE + TILE * member, TILE), TILE)]

    def peer_copy(slot, member, which, target):
        rows = quarter(slot, member)
        return remote(rows, rows, peer_send.at[slot, which], peer_recv.at[slot, member], peer_device(target))

    def pass_on(index):
        distance, up, other, slot, passes = step_of(index)

        @pl.when(index < 2)
        def _():
            for piece in range(4):
                def arrived(piece=piece):
                    remote(
                        own, stripes.at[slot, pl.ds(piece * PIECE, PIECE)], team_send.at[0, 0],
                        team_recv.at[other, piece], above,
                    ).wait_recv()

                if piece == 0:
                    pl.when(jnp.logical_not(first))(arrived)
                else:
                    arrived()
            thin_copy(slot, thin_send.at[slot], above).start()
            thin_copy(slot, thin_send_low.at[other], below).start()
            ring_copy(slot, ring_send.at[slot], above).start()
            ring_copy(slot, ring_send_low.at[other], below).start()

        @pl.when(index >= 2)
        def _():
            thin_copy(slot, thin_send.at[slot], above).wait_recv()

        @pl.when(passes & (up == 0))
        def _():
            thin_copy(slot, thin_send.at[slot], above).start()

        @pl.when(passes & (up == 1))
        def _():
            thin_copy(slot, thin_send.at[slot], below).start()

        @pl.when(index >= 2)
        def _():
            near, far = around(other)
            peer_copy(slot, depth, 0, far).start()
            peer_copy(slot, depth, 1, near).start()
            ring_copy(slot, ring_send.at[slot], above).wait_recv()

        @pl.when(passes & (up == 0))
        def _():
            ring_copy(slot, ring_send.at[slot], above).start()

        @pl.when(passes & (up == 1))
        def _():
            ring_copy(slot, ring_send.at[slot], below).start()

    def forward_step(count, carry):
        @pl.when(count < SECTIONS)
        def _():
            pass_on(count)

        @pl.when((count >= 3) & (count < SECTIONS + 1))
        def _():
            distance, up, other, slot, passes = step_of(count - 1)
            near, far = around(other)
            relay = peer_copy(slot, near, 2, far)
            relay.wait_recv()
            relay.start()

        @pl.when(count >= LAG)
        def _():
            index = count - LAG
            distance, up, other, slot, passes = step_of(index)
            section = section_of(slot)

            @pl.when(index >= 2)
            def _():
                near, far = around(other)
                peer_copy(slot, far, 0, near).wait_recv()
                peer_copy(slot, two, 0, near).wait_recv()

            load_of(section).wait()
            totals[...] += jnp.dot(blocks[section], stripes[slot], preferred_element_type=jnp.float32)

        return carry

    lax.fori_loop(0, SECTIONS + LAG, forward_step, 0)

    twin, cross = toggled(depth, 1), toggled(depth, 2)

    def piece_of(member):
        return pl.ds(pl.multiple_of(member * PIECE, PIECE), PIECE)

    def part_copy(which):
        source = parting if which == 2 else totals.at[piece_of(toggled(twin, 2) if which == 1 else twin)]
        return remote(
            source, parts.at[which], part_send.at[which], part_recv.at[which], (loop, cross if which == 2 else twin)
        )

    part_copy(1).start()
    part_copy(0).start()
    part_copy(1).wait_recv()
    parting[...] = totals[piece_of(cross), :] + parts[1]
    part_copy(2).start()
    part_copy(0).wait_recv()
    summed = totals[mine, :] + parts[0]
    part_copy(2).wait_recv()
    summed = summed + parts[2]

    aggregated_b = (norm_full * summed).astype(jnp.bfloat16)
    pre = jnp.dot(aggregated_b, weight[...], preferred_element_type=jnp.float32)
    sigma = jax.nn.sigmoid(pre)
    act[...] = pre * sigma
    signal = (cotangent[...] * (sigma * (1.0 + pre * (1.0 - sigma)))).astype(jnp.bfloat16)
    backed = lax.dot_general(weight[...], signal, (((1,), (1,)), ((), ())), preferred_element_type=jnp.float32)
    own_pushed[...] = (norm_row * backed).astype(jnp.bfloat16)

    def push_copy(offset):
        return remote(
            own_pushed, pushed.at[:, mine], push_send.at[offset], push_recv.at[offset], beside[offset]
        )

    for offset in range(3):
        push_copy(offset).start()
    pushed[:, mine] = own_pushed[...]
    terms[0] = lax.dot_general(aggregated_b, signal, (((0,), (0,)), ((), ())), preferred_element_type=jnp.float32)

    def term_copy(step):
        return remote(terms.at[step], other_terms.at[step], term_send.at[step], term_recv.at[step], partners[step])

    term_copy(0).start()
    for offset in range(3):
        source = pl.ds(pl.multiple_of(before[offset] * PIECE, PIECE), PIECE)
        remote(
            own_pushed, pushed.at[:, source], push_send.at[offset], push_recv.at[offset], beside[offset]
        ).wait_recv()

    def share_copy(other, piece):
        return remote(
            shares.at[other, piece], shared.at[other, depth], share_send.at[other, piece], share_recv.at[other, depth],
            owners[piece],
        )

    def back_copy(slot, target, recv, device):
        return remote(going.at[slot], target, back_send.at[slot], recv, device)

    def back_thin_copy(slot, target, recv, device):
        return remote(going_thin.at[slot], target, back_thin_send.at[slot], recv, device)

    def give_copy(slot, which, target):
        return remote(
            given.at[slot, which], taken.at[slot, which], give_send.at[slot, which], give_recv.at[slot, which],
            peer_device(target),
        )

    def lanes_of(member):
        return pl.ds(pl.multiple_of(WIDE + TILE * member, TILE), TILE)

    def multiply(index, held):
        distance, up, other, slot, passes = step_of(index)
        sums[held] = jnp.dot(pushed[...], blocks[section_of(slot)], preferred_element_type=jnp.float32)

        @pl.when(index >= 2)
        def _():
            near, far = around(other)
            given[slot, 0] = sums[held, :, lanes_of(two)].astype(jnp.bfloat16)
            give_copy(slot, 0, near).start()
            given[slot, 2] = sums[held, :, lanes_of(far)].astype(jnp.bfloat16)
            give_copy(slot, 2, far).start()

    def hand_on(index, held):
        distance, up, other, slot, passes = step_of(index)
        near, far = around(other)
        give_copy(slot, 0, near).wait_recv()
        given[slot, 1] = (sums[held, :, lanes_of(near)] + taken[slot, 0].astype(jnp.float32)).astype(jnp.bfloat16)
        give_copy(slot, 1, near).start()

    def reduce(index, held):
        distance, up, other, slot, passes = step_of(index)

        @pl.when(index >= 2)
        def _():
            near, far = around(other)
            for which in (1, 2):
                give_copy(slot, which, near).wait_recv()
                sums[held, :, thin] += taken[slot, which].astype(jnp.float32)

        @pl.when(passes | (index < 2))
        def _():
            back_thin_copy(slot, coming_thin.at[slot], back_thin_recv.at[slot], above).wait_recv()
            sums[held, :, thin] += coming_thin[slot].astype(jnp.float32)
            back_copy(slot, coming.at[slot], back_recv.at[slot], above).wait_recv()
            sums[held, :, wide] += coming[slot].astype(jnp.float32)

        @pl.when(index < 2)
        def _():
            back_thin_copy(slot, coming_thin_low.at[other], back_thin_recv_low.at[other], below).wait_recv()
            sums[held, :, thin] += coming_thin_low[other].astype(jnp.float32)
            back_copy(slot, coming_low.at[other], back_recv_low.at[other], below).wait_recv()
            sums[held, :, wide] += coming_low[other].astype(jnp.float32)
            for piece in range(4):
                shares[other, piece] = sums[held, :, pl.ds(piece * PIECE, PIECE)].astype(jnp.bfloat16)
                if piece == 0:
                    @pl.when(jnp.logical_not(first))
                    def _():
                        share_copy(other, 0).start()

                    @pl.when(first)
                    def _():
                        shared[other, 0] = shares[other, 0]
                else:
                    share_copy(other, piece).start()

        @pl.when(index >= 2)
        def _():
            going_thin[slot] = sums[held, :, thin].astype(jnp.bfloat16)
            going[slot] = sums[held, :, wide].astype(jnp.bfloat16)

        last_far = distance == 4

        @pl.when((index >= 2) & (((up == 0) & jnp.logical_not(last_far)) | (last_far & (other == 0))))
        def _():
            back_thin_copy(slot, coming_thin.at[slot], back_thin_recv.at[slot], below).start()
            back_copy(slot, coming.at[slot], back_recv.at[slot], below).start()

        @pl.when((index >= 2) & (((up == 1) & (distance > 1)) | (last_far & (other == 1))))
        def _():
            back_thin_copy(slot, coming_thin.at[slot], back_thin_recv.at[slot], above).start()
            back_copy(slot, coming.at[slot], back_recv.at[slot], above).start()

        @pl.when((index >= 2) & (up == 1) & (distance == 1))
        def _():
            back_thin_copy(slot, coming_thin_low.at[other], back_thin_recv_low.at[other], above).start()
            back_copy(slot, coming_low.at[other], back_recv_low.at[other], above).start()

    def backward_step(count, carry):
        @pl.when(count < SECTIONS)
        def _():
            multiply(SECTIONS - 1 - count, count % (LAG + 1))

        @pl.when((count >= 1) & (count < SECTIONS - 1))
        def _():
            hand_on(SECTIONS - count, (count - 1) % (LAG + 1))

        @pl.when(count >= LAG)
        def _():
            reduce(SECTIONS - 1 - (count - LAG), (count - LAG) % (LAG + 1))

        for step in range(1, 8):
            @pl.when(count == 2 * step)
            def _(step=step):
                term_copy(step - 1).wait_recv()
                terms[step] = terms[step - 1] + other_terms[step - 1]
                term_copy(step).start()

        return carry

    lax.fori_loop(0, SECTIONS + LAG, backward_step, 0)

    def shared_sum(other):
        gathered = jnp.zeros((FEAT, PIECE), jnp.float32)
        for member in range(4):
            def share_arrived(member=member):
                remote(
                    shares.at[0, 0], shared.at[other, member], share_send.at[0, 0], share_recv.at[other, member], above
                ).wait_recv()

            if member == 0:
                pl.when(jnp.logical_not(first))(share_arrived)
            else:
                share_arrived()
            gathered = gathered + shared[other, member].astype(jnp.float32)
        return gathered

    mate_out[...] = shared_sum(1).astype(jnp.bfloat16)
    mate_back = remote(mate_out, mate_in, mate_back_send, mate_back_recv, mate_device)
    mate_back.start()
    gathered = shared_sum(0)
    mate_back.wait_recv()
    gathered = gathered + mate_in[...].astype(jnp.float32)
    for tile in range(2):
        feature_grad[pl.ds(tile * TILE, TILE), :] = norm_full[tile * TILE:(tile + 1) * TILE] * lax.dot_general(
            order, gathered[:, tile * TILE:(tile + 1) * TILE], (((0,), (1,)), ((), ())),
            precision=lax.Precision.HIGHEST, preferred_element_type=jnp.float32,
        )

    term_copy(7).wait_recv()
    weight_grad[...] = terms[7] + other_terms[7]

    mate_copy.wait_send()
    mate_back.wait_send()
    for other in range(2):
        for index in range(4):
            def sent(other=other, index=index):
                team_copy(other, index).wait_send()
                share_copy(other, index).wait_send()

            if index == 0:
                pl.when(jnp.logical_not(first))(sent)
            else:
                sent()
    for offset in range(3):
        part_copy(offset).wait_send()
        push_copy(offset).wait_send()
    for step in range(8):
        term_copy(step).wait_send()

    def sent_step(index, carry):
        distance, up, other, slot, passes = step_of(index)

        @pl.when(index < 2)
        def _():
            ring_copy(slot, ring_send_low.at[other], below).wait_send()
            thin_copy(slot, thin_send_low.at[other], below).wait_send()

        @pl.when(passes | (index < 2))
        def _():
            ring_copy(slot, ring_send.at[slot], above).wait_send()
            thin_copy(slot, thin_send.at[slot], above).wait_send()

        @pl.when(index >= 2)
        def _():
            back_copy(slot, coming.at[slot], back_recv.at[slot], above).wait_send()
            back_thin_copy(slot, coming_thin.at[slot], back_thin_recv.at[slot], above).wait_send()
            for which in range(3):
                peer_copy(slot, depth, which, two).wait_send()
                give_copy(slot, which, two).wait_send()

        return carry

    lax.fori_loop(0, SECTIONS, sent_step, 0)


def finish_kernel(act, feature_grad, weight_grad, act_out, feature_out, weight_out):
    act_out[...] = act[...]
    feature_out[...] = feature_grad[...]
    weight_out[...] = weight_grad[...]


def finish(*results):
    vmem = pl.BlockSpec(memory_space=pltpu.VMEM)
    return pl.pallas_call(
        finish_kernel,
        out_shape=tuple(jax.ShapeDtypeStruct(value.shape, value.dtype) for value in results),
        in_specs=[vmem] * 3,
        out_specs=(vmem,) * 3,
        cost_estimate=pl.CostEstimate(flops=0, bytes_accessed=640_000, transcendentals=0),
    )(*results)


def layer(features, norm_row, weight, cotangent, dense):
    vmem = pl.BlockSpec(memory_space=pltpu.VMEM)
    dma = pltpu.SemaphoreType.DMA
    bf16, f32 = jnp.bfloat16, jnp.float32
    return pl.pallas_call(
        layer_kernel,
        out_shape=(
            jax.ShapeDtypeStruct((PIECE, FEAT), f32),
            jax.ShapeDtypeStruct((PIECE, FEAT), f32),
            jax.ShapeDtypeStruct((FEAT, FEAT), f32),
        ),
        in_specs=[vmem, vmem, vmem, vmem, pl.BlockSpec(memory_space=pl.ANY)],
        out_specs=(vmem, vmem, vmem),
        scratch_shapes=[
            pltpu.VMEM((SECTIONS, STRIPE, STRIPE), bf16),
            pltpu.VMEM((SECTIONS, STRIPE, FEAT), bf16),
            pltpu.VMEM((PIECE, FEAT), bf16),
            pltpu.VMEM((PIECE, FEAT), bf16),
            pltpu.VMEM((FEAT, PIECE), bf16),
            pltpu.VMEM((FEAT, PIECE), bf16),
            pltpu.VMEM((STRIPE, FEAT), f32),
            pltpu.VMEM((PIECE, FEAT), f32),
            pltpu.VMEM((3, PIECE, FEAT), f32),
            pltpu.VMEM((FEAT, STRIPE), bf16),
            pltpu.VMEM((FEAT, PIECE), bf16),
            pltpu.VMEM((LAG + 1, FEAT, STRIPE), f32),
            pltpu.VMEM((SECTIONS, FEAT, WIDE), bf16),
            pltpu.VMEM((SECTIONS, FEAT, TILE), bf16),
            pltpu.VMEM((SECTIONS, FEAT, WIDE), bf16),
            pltpu.VMEM((SECTIONS, FEAT, TILE), bf16),
            pltpu.VMEM((2, FEAT, WIDE), bf16),
            pltpu.VMEM((2, FEAT, TILE), bf16),
            pltpu.VMEM((SECTIONS, 3, FEAT, TILE), bf16),
            pltpu.VMEM((SECTIONS, 3, FEAT, TILE), bf16),
            pltpu.VMEM((2, 4, FEAT, PIECE), bf16),
            pltpu.VMEM((2, 4, FEAT, PIECE), bf16),
            pltpu.VMEM((8, FEAT, FEAT), f32),
            pltpu.VMEM((8, FEAT, FEAT), f32),
            dma((SECTIONS,)), dma, dma, dma, dma,
            dma((2, 4)), dma((2, 4)), dma((SECTIONS,)), dma((2,)), dma((SECTIONS,)),
            dma((SECTIONS,)), dma((2,)), dma((SECTIONS,)), dma((SECTIONS, 3)), dma((SECTIONS, 4)),
            dma((3,)), dma((3,)), dma((3,)), dma((3,)),
            dma((SECTIONS,)), dma((SECTIONS,)), dma((2,)), dma((SECTIONS,)), dma((SECTIONS,)), dma((2,)),
            dma((SECTIONS, 3)), dma((SECTIONS, 3)),
            dma((2, 4)), dma((2, 4)), dma((8,)), dma((8,)),
        ],
        compiler_params=pltpu.CompilerParams(
            collective_id=0, has_side_effects=True, vmem_limit_bytes=60 * 1024 * 1024
        ),
        cost_estimate=pl.CostEstimate(flops=9_000_000_000, bytes_accessed=34_000_000, transcendentals=32768),
    )(features, norm_row, weight, cotangent, dense)


def per_device(features, norm_scale, weight, cotangent, tile_rows, tile_cols, tile_masks, tile_counts):
    dense = dense_blocks(tile_rows[0, 0], tile_cols[0, 0], tile_counts[0, 0], tile_masks[0, 0])
    return finish(*layer(features, norm_scale.reshape(1, -1), weight, cotangent, dense))


def solution(mesh):
    return jax.shard_map(
        per_device,
        mesh=mesh,
        in_specs=(
            P(("loop", "depth"), None),
            P(("loop", "depth")),
            P(),
            P(("loop", "depth"), None),
            P("loop", "depth", None, None),
            P("loop", "depth", None, None),
            P("loop", "depth", None, None, None),
            P("loop", "depth", None),
        ),
        out_specs=(P(("loop", "depth"), None), P(("loop", "depth"), None), P()),
        check_vma=False,
    )
```

```python
import jax
import jax.numpy as jnp
from jax import lax
from jax.experimental import pallas as pl
from jax.experimental.pallas import tpu as pltpu
from jax.sharding import PartitionSpec as P

TILE = 128
SECTIONS = 16
CAP = 48
STRIPE = 1024
PIECE = 256
FEAT = 128
RING = 8
UNROLL = 4
WIDE = 512
LAG = 3
MESH = pl.DeviceIdType.MESH


def dense_kernel(rows, cols, counts, masks, out, words, packed, sem):
    lane = lax.broadcasted_iota(jnp.int32, (8, 128), 1)
    row = lax.broadcasted_iota(jnp.int32, (8, 128), 0)
    place = row * 16 + lax.rem(lane, 16)
    bit = lax.div(lane, 16)

    def fetch(section, held):
        return pltpu.make_async_copy(masks.at[section], words.at[held], sem.at[held])

    fetch(0, 0).start()
    packed[pl.ds(CAP, UNROLL)] = jnp.zeros((UNROLL, 4, 128), jnp.int32)

    def near_of(group):
        return [
            jnp.take_along_axis(
                jnp.broadcast_to(packed[group * UNROLL + index, pl.ds(part, 1), :], (8, 128)),
                place, axis=1, mode="promise_in_bounds",
            )
            for index in range(UNROLL) for part in range(4)
        ]

    def section_step(section, carry):
        held = section % 2

        @pl.when(section + 1 < SECTIONS)
        def _():
            fetch(section + 1, (section + 1) % 2).start()

        out[section] = jnp.zeros((STRIPE, STRIPE), jnp.bfloat16)
        fetch(section, held).wait()
        for eight in range(CAP // 8):
            slots = pl.ds(eight * 8, 8)
            for part in range(4):
                value = words[held, slots, pl.ds(part * 512, 128)]
                for step in range(1, 4):
                    value = value | (words[held, slots, pl.ds(part * 512 + step * 128, 128)] << (8 * step))
                packed[slots, part, :] = value
        live_count = counts[section]

        def group_step(group, nears):
            later = near_of(group + 1)
            for index in range(UNROLL):
                slot = group * UNROLL + index
                live = jnp.where(slot < live_count, 1, 0)
                strips = [
                    ((nears[4 * index + part] >> (bit + 8 * step)) & live).astype(jnp.float32)
                    for part in range(4) for step in range(4)
                ]
                tile = jnp.concatenate(strips, axis=0).astype(jnp.bfloat16)
                top = pl.multiple_of(rows[section, slot] * TILE, TILE)
                left = pl.multiple_of(cols[section, slot] * TILE, TILE)
                out[section, pl.ds(top, TILE), pl.ds(left, TILE)] += tile
            return later

        lax.fori_loop(0, (live_count + UNROLL - 1) // UNROLL, group_step, near_of(0))
        return carry

    lax.fori_loop(0, SECTIONS, section_step, 0)


def dense_blocks(tile_rows, tile_cols, tile_counts, tile_masks):
    smem = pl.BlockSpec(memory_space=pltpu.SMEM)
    return pl.pallas_call(
        dense_kernel,
        out_shape=pltpu.VMEM((SECTIONS, STRIPE, STRIPE), jnp.bfloat16),
        in_specs=[smem, smem, smem, pl.BlockSpec(memory_space=pl.ANY)],
        out_specs=pl.BlockSpec(memory_space=pltpu.VMEM),
        scratch_shapes=[
            pltpu.VMEM((2, CAP, 2048), jnp.int32),
            pltpu.VMEM((CAP + UNROLL, 4, 128), jnp.int32),
            pltpu.SemaphoreType.DMA((2,)),
        ],
        compiler_params=pltpu.CompilerParams(vmem_limit_bytes=28 * 1024 * 1024),
        cost_estimate=pl.CostEstimate(flops=50_000_000, bytes_accessed=8_000_000, transcendentals=0),
    )(tile_rows, tile_cols, tile_counts, tile_masks)


def layer_kernel(
    features, norm, weight, cotangent, blocks, act, feature_grad, weight_grad,
    stripes, own, mate, mate_out, mate_in, totals, parting, parts, pushed, own_pushed, sums, going, going_thin, coming, coming_thin, coming_low,
    coming_thin_low, given, taken, shares, shared, terms, other_terms,
    mate_send, mate_recv, mate_back_send, mate_back_recv, team_send, team_recv, ring_send, ring_send_low, ring_recv, thin_send, thin_send_low, thin_recv, peer_send,
    peer_recv, part_send, part_recv, push_send, push_recv, back_send, back_recv, back_recv_low, back_thin_send,
    back_thin_recv, back_thin_recv_low, give_send, give_recv, share_send, share_recv, term_send, term_recv,
):
    loop = lax.axis_index("loop")
    depth = lax.axis_index("depth")
    z = loop // 8
    half = (loop // 4) % 2
    y = loop % 4
    node = loop // 4
    kind = (y - depth + 4) % 4
    first = depth == 0

    def remote(source, target, send, recv, device):
        return pltpu.make_async_remote_copy(
            src_ref=source, dst_ref=target, send_sem=send, recv_sem=recv, device_id=device, device_id_type=MESH
        )

    def toggled(value, bit):
        return value + bit - 2 * bit * ((value // bit) % 2)

    above = (((z + 1) % RING) * 8 + loop % 8, depth)
    below = (((z + RING - 1) % RING) * 8 + loop % 8, depth)
    mate_node = z * 2 + 1 - half
    mate_device = (mate_node * 4 + y, depth)
    team = [(node * 4 + (y + member) % 4, member) for member in range(4)]
    owners = [(node * 4 + kind, piece) for piece in range(4)]
    beside = [(loop, (depth + offset) % 4) for offset in range(1, 4)]
    two = (depth + 2) % 4

    def peer_device(member):
        return (node * 4 + (kind + member) % 4, member)

    def around(other):
        return (depth + 3 + 2 * other) % 4, (depth + 1 + 2 * other) % 4

    before = [(depth + 4 - offset) % 4 for offset in range(1, 4)]
    partners = [
        (toggled(loop, 32), depth), (toggled(loop, 16), depth), (toggled(loop, 8), depth), (toggled(loop, 2), depth),
        (toggled(loop, 1), depth), (toggled(loop, 4), depth), (loop, toggled(depth, 2)), (loop, toggled(depth, 1)),
    ]

    def section_of(slot):
        return ((loop - depth - kind - 4 * slot + 128) // 4) % SECTIONS

    def step_of(index):
        distance = (index + 2) // 4
        up = ((index + 2) // 2) % 2
        other = index % 2
        slot = ((z + RING - distance + 2 * distance * up) % RING) * 2 + (half + other) % 2
        passes = (index >= 2) & ((distance < 3) | ((distance == 3) & (other == up)))
        return distance, up, other, slot, passes

    barrier = pltpu.get_barrier_semaphore()
    for device in [above, below] + beside + [peer_device((depth + offset) % 4) for offset in range(1, 4)] + [mate_device, partners[0], partners[1], partners[3], partners[4]]:
        pl.semaphore_signal(barrier, inc=1, device_id=device, device_id_type=MESH)
    for index in range(4):
        def greet(index=index):
            pl.semaphore_signal(barrier, inc=1, device_id=team[index], device_id_type=MESH)
            pl.semaphore_signal(barrier, inc=1, device_id=owners[index], device_id_type=MESH)

        if index == 0:
            pl.when(jnp.logical_not(first))(greet)
        else:
            greet()

    order_row = lax.broadcasted_iota(jnp.int32, (TILE, TILE), 0)
    order_col = lax.broadcasted_iota(jnp.int32, (TILE, TILE), 1)
    order = jnp.where(order_col == 8 * (order_row % 16) + order_row // 16, 1.0, 0.0)
    norm_row = norm[...]
    norm_full = jnp.broadcast_to(norm_row, (FEAT, PIECE)).T
    scaled = (norm_full * features[...]).astype(jnp.bfloat16)
    for tile in range(2):
        own[pl.ds(tile * TILE, TILE), :] = jnp.dot(
            order.astype(jnp.bfloat16), scaled[tile * TILE:(tile + 1) * TILE], preferred_element_type=jnp.float32
        ).astype(jnp.bfloat16)

    pl.semaphore_wait(barrier, jnp.where(first, 19, 21))

    mine = pl.ds(pl.multiple_of(depth * PIECE, PIECE), PIECE)

    def team_copy(other, member):
        return remote(
            own if other == 0 else mate, stripes.at[node if other == 0 else mate_node, mine],
            team_send.at[other, member], team_recv.at[other, depth], team[member],
        )

    mate_copy = remote(own, mate, mate_send, mate_recv, mate_device)
    mate_copy.start()
    for other in range(2):
        if other == 1:
            mate_copy.wait_recv()
        for member in range(4):
            if member == 0:
                @pl.when(jnp.logical_not(first))
                def _(other=other):
                    team_copy(other, 0).start()
            else:
                team_copy(other, member).start()

    @pl.when(first)
    def _():
        stripes[node, 0:PIECE, :] = own[...]
        stripes[mate_node, 0:PIECE, :] = mate[...]

    totals[...] = jnp.zeros_like(totals)

    wide = pl.ds(0, WIDE)
    thin = pl.ds(pl.multiple_of(WIDE + TILE * depth, TILE), TILE)

    def ring_copy(slot, send, device):
        rows = stripes.at[slot, wide]
        return remote(rows, rows, send, ring_recv.at[slot], device)

    def thin_copy(slot, send, device):
        rows = stripes.at[slot, thin]
        return remote(rows, rows, send, thin_recv.at[slot], device)

    def quarter(slot, member):
        return stripes.at[slot, pl.ds(pl.multiple_of(WIDE + TILE * member, TILE), TILE)]

    def peer_copy(slot, member, which, target):
        rows = quarter(slot, member)
        return remote(rows, rows, peer_send.at[slot, which], peer_recv.at[slot, member], peer_device(target))

    def pass_on(index):
        distance, up, other, slot, passes = step_of(index)

        @pl.when(index < 2)
        def _():
            for piece in range(4):
                def arrived(piece=piece):
                    remote(
                        own, stripes.at[slot, pl.ds(piece * PIECE, PIECE)], team_send.at[0, 0],
                        team_recv.at[other, piece], above,
                    ).wait_recv()

                if piece == 0:
                    pl.when(jnp.logical_not(first))(arrived)
                else:
                    arrived()
            thin_copy(slot, thin_send.at[slot], above).start()
            thin_copy(slot, thin_send_low.at[other], below).start()
            ring_copy(slot, ring_send.at[slot], above).start()
            ring_copy(slot, ring_send_low.at[other], below).start()

        @pl.when(index >= 2)
        def _():
            thin_copy(slot, thin_send.at[slot], above).wait_recv()

        @pl.when(passes & (up == 0))
        def _():
            thin_copy(slot, thin_send.at[slot], above).start()

        @pl.when(passes & (up == 1))
        def _():
            thin_copy(slot, thin_send.at[slot], below).start()

        @pl.when(index >= 2)
        def _():
            near, far = around(other)
            peer_copy(slot, depth, 0, far).start()
            peer_copy(slot, depth, 1, near).start()
            ring_copy(slot, ring_send.at[slot], above).wait_recv()

        @pl.when(passes & (up == 0))
        def _():
            ring_copy(slot, ring_send.at[slot], above).start()

        @pl.when(passes & (up == 1))
        def _():
            ring_copy(slot, ring_send.at[slot], below).start()

    def forward_step(count, carry):
        @pl.when(count < SECTIONS)
        def _():
            pass_on(count)

        @pl.when((count >= 3) & (count < SECTIONS + 1))
        def _():
            distance, up, other, slot, passes = step_of(count - 1)
            near, far = around(other)
            relay = peer_copy(slot, near, 2, far)
            relay.wait_recv()
            relay.start()

        @pl.when(count >= LAG)
        def _():
            index = count - LAG
            distance, up, other, slot, passes = step_of(index)
            section = section_of(slot)

            @pl.when(index >= 2)
            def _():
                near, far = around(other)
                peer_copy(slot, far, 0, near).wait_recv()
                peer_copy(slot, two, 0, near).wait_recv()

            totals[...] += jnp.dot(blocks[section], stripes[slot], preferred_element_type=jnp.float32)

        return carry

    lax.fori_loop(0, SECTIONS + LAG, forward_step, 0)

    twin, cross = toggled(depth, 1), toggled(depth, 2)

    def piece_of(member):
        return pl.ds(pl.multiple_of(member * PIECE, PIECE), PIECE)

    def part_copy(which):
        source = parting if which == 2 else totals.at[piece_of(toggled(twin, 2) if which == 1 else twin)]
        return remote(
            source, parts.at[which], part_send.at[which], part_recv.at[which], (loop, cross if which == 2 else twin)
        )

    part_copy(1).start()
    part_copy(0).start()
    part_copy(1).wait_recv()
    parting[...] = totals[piece_of(cross), :] + parts[1]
    part_copy(2).start()
    part_copy(0).wait_recv()
    summed = totals[mine, :] + parts[0]
    part_copy(2).wait_recv()
    summed = summed + parts[2]

    aggregated_b = (norm_full * summed).astype(jnp.bfloat16)
    pre = jnp.dot(aggregated_b, weight[...], preferred_element_type=jnp.float32)
    sigma = jax.nn.sigmoid(pre)
    act[...] = pre * sigma
    signal = (cotangent[...] * (sigma * (1.0 + pre * (1.0 - sigma)))).astype(jnp.bfloat16)
    backed = lax.dot_general(weight[...], signal, (((1,), (1,)), ((), ())), preferred_element_type=jnp.float32)
    own_pushed[...] = (norm_row * backed).astype(jnp.bfloat16)

    def push_copy(offset):
        return remote(
            own_pushed, pushed.at[:, mine], push_send.at[offset], push_recv.at[offset], beside[offset]
        )

    for offset in range(3):
        push_copy(offset).start()
    pushed[:, mine] = own_pushed[...]
    terms[0] = lax.dot_general(aggregated_b, signal, (((0,), (0,)), ((), ())), preferred_element_type=jnp.float32)

    def term_copy(step):
        return remote(terms.at[step], other_terms.at[step], term_send.at[step], term_recv.at[step], partners[step])

    term_copy(0).start()
    for offset in range(3):
        source = pl.ds(pl.multiple_of(before[offset] * PIECE, PIECE), PIECE)
        remote(
            own_pushed, pushed.at[:, source], push_send.at[offset], push_recv.at[offset], beside[offset]
        ).wait_recv()

    def share_copy(other, piece):
        return remote(
            shares.at[other, piece], shared.at[other, depth], share_send.at[other, piece], share_recv.at[other, depth],
            owners[piece],
        )

    def back_copy(slot, target, recv, device):
        return remote(going.at[slot], target, back_send.at[slot], recv, device)

    def back_thin_copy(slot, target, recv, device):
        return remote(going_thin.at[slot], target, back_thin_send.at[slot], recv, device)

    def give_copy(slot, which, target):
        return remote(
            given.at[slot, which], taken.at[slot, which], give_send.at[slot, which], give_recv.at[slot, which],
            peer_device(target),
        )

    def lanes_of(member):
        return pl.ds(pl.multiple_of(WIDE + TILE * member, TILE), TILE)

    def multiply(index, held):
        distance, up, other, slot, passes = step_of(index)
        sums[held] = jnp.dot(pushed[...], blocks[section_of(slot)], preferred_element_type=jnp.float32)

        @pl.when(index >= 2)
        def _():
            near, far = around(other)
            given[slot, 0] = sums[held, :, lanes_of(two)].astype(jnp.bfloat16)
            give_copy(slot, 0, near).start()
            given[slot, 2] = sums[held, :, lanes_of(far)].astype(jnp.bfloat16)
            give_copy(slot, 2, far).start()

    def hand_on(index, held):
        distance, up, other, slot, passes = step_of(index)
        near, far = around(other)
        give_copy(slot, 0, near).wait_recv()
        given[slot, 1] = (sums[held, :, lanes_of(near)] + taken[slot, 0].astype(jnp.float32)).astype(jnp.bfloat16)
        give_copy(slot, 1, near).start()

    def share(other, held, pieces):
        for piece in pieces:
            shares[other, piece] = sums[held, :, pl.ds(piece * PIECE, PIECE)].astype(jnp.bfloat16)
            if piece == 0:
                @pl.when(jnp.logical_not(first))
                def _():
                    share_copy(other, 0).start()

                @pl.when(first)
                def _():
                    shared[other, 0] = shares[other, 0]
            else:
                share_copy(other, piece).start()

    def send_back(index, copy, main, low):
        distance, up, other, slot, passes = step_of(index)
        last_far = distance == 4

        @pl.when((index >= 2) & (((up == 0) & jnp.logical_not(last_far)) | (last_far & (other == 0))))
        def _():
            copy(slot, main[0].at[slot], main[1].at[slot], below).start()

        @pl.when((index >= 2) & (((up == 1) & (distance > 1)) | (last_far & (other == 1))))
        def _():
            copy(slot, main[0].at[slot], main[1].at[slot], above).start()

        @pl.when((index >= 2) & (up == 1) & (distance == 1))
        def _():
            copy(slot, low[0].at[other], low[1].at[other], above).start()

    def reduce_wide(index, held):
        distance, up, other, slot, passes = step_of(index)

        @pl.when(passes | (index < 2))
        def _():
            back_copy(slot, coming.at[slot], back_recv.at[slot], above).wait_recv()
            sums[held, :, wide] += coming[slot].astype(jnp.float32)

        @pl.when(index < 2)
        def _():
            back_copy(slot, coming_low.at[other], back_recv_low.at[other], below).wait_recv()
            sums[held, :, wide] += coming_low[other].astype(jnp.float32)
            share(other, held, (0, 1))

        @pl.when(index >= 2)
        def _():
            going[slot] = sums[held, :, wide].astype(jnp.bfloat16)

        send_back(index, back_copy, (coming, back_recv), (coming_low, back_recv_low))

    def reduce_thin(index, held):
        distance, up, other, slot, passes = step_of(index)

        @pl.when(index >= 2)
        def _():
            near, far = around(other)
            for which in (1, 2):
                give_copy(slot, which, near).wait_recv()
                sums[held, :, thin] += taken[slot, which].astype(jnp.float32)

        @pl.when(passes | (index < 2))
        def _():
            back_thin_copy(slot, coming_thin.at[slot], back_thin_recv.at[slot], above).wait_recv()
            sums[held, :, thin] += coming_thin[slot].astype(jnp.float32)

        @pl.when(index < 2)
        def _():
            back_thin_copy(slot, coming_thin_low.at[other], back_thin_recv_low.at[other], below).wait_recv()
            sums[held, :, thin] += coming_thin_low[other].astype(jnp.float32)
            share(other, held, (2, 3))

        @pl.when(index >= 2)
        def _():
            going_thin[slot] = sums[held, :, thin].astype(jnp.bfloat16)

        send_back(index, back_thin_copy, (coming_thin, back_thin_recv), (coming_thin_low, back_thin_recv_low))

    def backward_step(count, carry):
        @pl.when(count < SECTIONS)
        def _():
            multiply(SECTIONS - 1 - count, count % (LAG + 1))

        @pl.when((count >= 1) & (count < SECTIONS + 1))
        def _():
            reduce_wide(SECTIONS - count, (count - 1) % (LAG + 1))

        @pl.when((count >= 2) & (count < SECTIONS))
        def _():
            hand_on(SECTIONS + 1 - count, (count - 2) % (LAG + 1))

        @pl.when(count >= LAG)
        def _():
            reduce_thin(SECTIONS - 1 - (count - LAG), (count - LAG) % (LAG + 1))

        for step in range(1, 8):
            @pl.when(count == (2, 4, 6, 9, 12, 15, 18)[step - 1])
            def _(step=step):
                term_copy(step - 1).wait_recv()
                terms[step] = terms[step - 1] + other_terms[step - 1]
                term_copy(step).start()

        return carry

    lax.fori_loop(0, SECTIONS + LAG, backward_step, 0)

    def shared_sum(other):
        gathered = jnp.zeros((FEAT, PIECE), jnp.float32)
        for member in range(4):
            def share_arrived(member=member):
                remote(
                    shares.at[0, 0], shared.at[other, member], share_send.at[0, 0], share_recv.at[other, member], above
                ).wait_recv()

            if member == 0:
                pl.when(jnp.logical_not(first))(share_arrived)
            else:
                share_arrived()
            gathered = gathered + shared[other, member].astype(jnp.float32)
        return gathered

    mate_out[...] = shared_sum(1).astype(jnp.bfloat16)
    mate_back = remote(mate_out, mate_in, mate_back_send, mate_back_recv, mate_device)
    mate_back.start()
    gathered = shared_sum(0)
    mate_back.wait_recv()
    gathered = gathered + mate_in[...].astype(jnp.float32)
    for tile in range(2):
        feature_grad[pl.ds(tile * TILE, TILE), :] = norm_full[tile * TILE:(tile + 1) * TILE] * lax.dot_general(
            order, gathered[:, tile * TILE:(tile + 1) * TILE], (((0,), (1,)), ((), ())),
            precision=lax.Precision.HIGHEST, preferred_element_type=jnp.float32,
        )

    term_copy(7).wait_recv()
    weight_grad[...] = terms[7] + other_terms[7]

    mate_copy.wait_send()
    mate_back.wait_send()
    for other in range(2):
        for index in range(4):
            def sent(other=other, index=index):
                team_copy(other, index).wait_send()
                share_copy(other, index).wait_send()

            if index == 0:
                pl.when(jnp.logical_not(first))(sent)
            else:
                sent()
    for offset in range(3):
        part_copy(offset).wait_send()
        push_copy(offset).wait_send()
    for step in range(8):
        term_copy(step).wait_send()

    def sent_step(index, carry):
        distance, up, other, slot, passes = step_of(index)

        @pl.when(index < 2)
        def _():
            ring_copy(slot, ring_send_low.at[other], below).wait_send()
            thin_copy(slot, thin_send_low.at[other], below).wait_send()

        @pl.when(passes | (index < 2))
        def _():
            ring_copy(slot, ring_send.at[slot], above).wait_send()
            thin_copy(slot, thin_send.at[slot], above).wait_send()

        @pl.when(index >= 2)
        def _():
            back_copy(slot, coming.at[slot], back_recv.at[slot], above).wait_send()
            back_thin_copy(slot, coming_thin.at[slot], back_thin_recv.at[slot], above).wait_send()
            for which in range(3):
                peer_copy(slot, depth, which, two).wait_send()
                give_copy(slot, which, two).wait_send()

        return carry

    lax.fori_loop(0, SECTIONS, sent_step, 0)


def finish_kernel(act, feature_grad, weight_grad, act_out, feature_out, weight_out):
    act_out[...] = act[...]
    feature_out[...] = feature_grad[...]
    weight_out[...] = weight_grad[...]


def finish(*results):
    vmem = pl.BlockSpec(memory_space=pltpu.VMEM)
    return pl.pallas_call(
        finish_kernel,
        out_shape=tuple(jax.ShapeDtypeStruct(value.shape, value.dtype) for value in results),
        in_specs=[vmem] * 3,
        out_specs=(vmem,) * 3,
        compiler_params=pltpu.CompilerParams(vmem_limit_bytes=60 * 1024 * 1024),
        cost_estimate=pl.CostEstimate(flops=0, bytes_accessed=640_000, transcendentals=0),
    )(*results)


def layer(features, norm_row, weight, cotangent, dense):
    vmem = pl.BlockSpec(memory_space=pltpu.VMEM)
    dma = pltpu.SemaphoreType.DMA
    bf16, f32 = jnp.bfloat16, jnp.float32
    return pl.pallas_call(
        layer_kernel,
        out_shape=(
            jax.ShapeDtypeStruct((PIECE, FEAT), f32),
            jax.ShapeDtypeStruct((PIECE, FEAT), f32),
            jax.ShapeDtypeStruct((FEAT, FEAT), f32),
        ),
        in_specs=[vmem, vmem, vmem, vmem, vmem],
        out_specs=(vmem, vmem, vmem),
        scratch_shapes=[
            pltpu.VMEM((SECTIONS, STRIPE, FEAT), bf16),
            pltpu.VMEM((PIECE, FEAT), bf16),
            pltpu.VMEM((PIECE, FEAT), bf16),
            pltpu.VMEM((FEAT, PIECE), bf16),
            pltpu.VMEM((FEAT, PIECE), bf16),
            pltpu.VMEM((STRIPE, FEAT), f32),
            pltpu.VMEM((PIECE, FEAT), f32),
            pltpu.VMEM((3, PIECE, FEAT), f32),
            pltpu.VMEM((FEAT, STRIPE), bf16),
            pltpu.VMEM((FEAT, PIECE), bf16),
            pltpu.VMEM((LAG + 1, FEAT, STRIPE), f32),
            pltpu.VMEM((SECTIONS, FEAT, WIDE), bf16),
            pltpu.VMEM((SECTIONS, FEAT, TILE), bf16),
            pltpu.VMEM((SECTIONS, FEAT, WIDE), bf16),
            pltpu.VMEM((SECTIONS, FEAT, TILE), bf16),
            pltpu.VMEM((2, FEAT, WIDE), bf16),
            pltpu.VMEM((2, FEAT, TILE), bf16),
            pltpu.VMEM((SECTIONS, 3, FEAT, TILE), bf16),
            pltpu.VMEM((SECTIONS, 3, FEAT, TILE), bf16),
            pltpu.VMEM((2, 4, FEAT, PIECE), bf16),
            pltpu.VMEM((2, 4, FEAT, PIECE), bf16),
            pltpu.VMEM((8, FEAT, FEAT), f32),
            pltpu.VMEM((8, FEAT, FEAT), f32),
            dma, dma, dma, dma,
            dma((2, 4)), dma((2, 4)), dma((SECTIONS,)), dma((2,)), dma((SECTIONS,)),
            dma((SECTIONS,)), dma((2,)), dma((SECTIONS,)), dma((SECTIONS, 3)), dma((SECTIONS, 4)),
            dma((3,)), dma((3,)), dma((3,)), dma((3,)),
            dma((SECTIONS,)), dma((SECTIONS,)), dma((2,)), dma((SECTIONS,)), dma((SECTIONS,)), dma((2,)),
            dma((SECTIONS, 3)), dma((SECTIONS, 3)),
            dma((2, 4)), dma((2, 4)), dma((8,)), dma((8,)),
        ],
        compiler_params=pltpu.CompilerParams(
            collective_id=0, has_side_effects=True, vmem_limit_bytes=30 * 1024 * 1024
        ),
        cost_estimate=pl.CostEstimate(flops=9_000_000_000, bytes_accessed=34_000_000, transcendentals=32768),
    )(features, norm_row, weight, cotangent, pltpu.with_memory_space_constraint(dense, pltpu.VMEM))


def per_device(features, norm_scale, weight, cotangent, tile_rows, tile_cols, tile_masks, tile_counts):
    dense = dense_blocks(tile_rows[0, 0], tile_cols[0, 0], tile_counts[0, 0], tile_masks[0, 0])
    return finish(*layer(features, norm_scale.reshape(1, -1), weight, cotangent, dense))


def solution(mesh):
    return jax.shard_map(
        per_device,
        mesh=mesh,
        in_specs=(
            P(("loop", "depth"), None),
            P(("loop", "depth")),
            P(),
            P(("loop", "depth"), None),
            P("loop", "depth", None, None),
            P("loop", "depth", None, None),
            P("loop", "depth", None, None, None),
            P("loop", "depth", None),
        ),
        out_specs=(P(("loop", "depth"), None), P(("loop", "depth"), None), P()),
        check_vma=False,
    )
```

```python
import jax
import jax.numpy as jnp
from jax import lax
from jax.experimental import pallas as pl
from jax.experimental.pallas import tpu as pltpu
from jax.sharding import PartitionSpec as P

TILE = 128
SECTIONS = 16
CAP = 48
STRIPE = 1024
PIECE = 256
FEAT = 128
RING = 8
UNROLL = 4
WIDE = 512
LAG = 4
MESH = pl.DeviceIdType.MESH


def dense_kernel(rows, cols, counts, masks, out, words, packed, sem):
    lane = lax.broadcasted_iota(jnp.int32, (8, 128), 1)
    row = lax.broadcasted_iota(jnp.int32, (8, 128), 0)
    place = row * 16 + lax.rem(lane, 16)
    bit = lax.div(lane, 16)

    def fetch(section, held):
        return pltpu.make_async_copy(masks.at[section], words.at[held], sem.at[held])

    fetch(0, 0).start()
    packed[pl.ds(CAP, UNROLL)] = jnp.zeros((UNROLL, 4, 128), jnp.int32)

    def near_of(group):
        return [
            jnp.take_along_axis(
                jnp.broadcast_to(packed[group * UNROLL + index, pl.ds(part, 1), :], (8, 128)),
                place, axis=1, mode="promise_in_bounds",
            )
            for index in range(UNROLL) for part in range(4)
        ]

    def section_step(section, carry):
        held = section % 2

        @pl.when(section + 1 < SECTIONS)
        def _():
            fetch(section + 1, (section + 1) % 2).start()

        out[section] = jnp.zeros((STRIPE, STRIPE), jnp.bfloat16)
        fetch(section, held).wait()
        for eight in range(CAP // 8):
            slots = pl.ds(eight * 8, 8)
            for part in range(4):
                value = words[held, slots, pl.ds(part * 512, 128)]
                for step in range(1, 4):
                    value = value | (words[held, slots, pl.ds(part * 512 + step * 128, 128)] << (8 * step))
                packed[slots, part, :] = value
        live_count = counts[section]

        def group_step(group, nears):
            later = near_of(group + 1)
            for index in range(UNROLL):
                slot = group * UNROLL + index
                live = jnp.where(slot < live_count, 1, 0)
                strips = [
                    ((nears[4 * index + part] >> (bit + 8 * step)) & live).astype(jnp.float32)
                    for part in range(4) for step in range(4)
                ]
                tile = jnp.concatenate(strips, axis=0).astype(jnp.bfloat16)
                top = pl.multiple_of(rows[section, slot] * TILE, TILE)
                left = pl.multiple_of(cols[section, slot] * TILE, TILE)
                out[section, pl.ds(top, TILE), pl.ds(left, TILE)] += tile
            return later

        lax.fori_loop(0, (live_count + UNROLL - 1) // UNROLL, group_step, near_of(0))
        return carry

    lax.fori_loop(0, SECTIONS, section_step, 0)


def dense_blocks(tile_rows, tile_cols, tile_counts, tile_masks):
    smem = pl.BlockSpec(memory_space=pltpu.SMEM)
    return pl.pallas_call(
        dense_kernel,
        out_shape=pltpu.VMEM((SECTIONS, STRIPE, STRIPE), jnp.bfloat16),
        in_specs=[smem, smem, smem, pl.BlockSpec(memory_space=pl.ANY)],
        out_specs=pl.BlockSpec(memory_space=pltpu.VMEM),
        scratch_shapes=[
            pltpu.VMEM((2, CAP, 2048), jnp.int32),
            pltpu.VMEM((CAP + UNROLL, 4, 128), jnp.int32),
            pltpu.SemaphoreType.DMA((2,)),
        ],
        compiler_params=pltpu.CompilerParams(vmem_limit_bytes=28 * 1024 * 1024),
        cost_estimate=pl.CostEstimate(flops=50_000_000, bytes_accessed=8_000_000, transcendentals=0),
    )(tile_rows, tile_cols, tile_counts, tile_masks)


def layer_kernel(
    features, norm, weight, cotangent, blocks, act, feature_grad, weight_grad,
    stripes, own, mate, mate_out, mate_in, totals, parting, parts, pushed, own_pushed, sums, going, going_thin, coming, coming_thin, coming_low,
    coming_thin_low, given, taken, shares, shared, terms, other_terms,
    mate_send, mate_recv, mate_back_send, mate_back_recv, team_send, team_recv, ring_send, ring_send_low, ring_recv, thin_send, thin_send_low, thin_recv, peer_send,
    peer_recv, part_send, part_recv, push_send, push_recv, back_send, back_recv, back_recv_low, back_thin_send,
    back_thin_recv, back_thin_recv_low, give_send, give_recv, share_send, share_recv, term_send, term_recv,
):
    loop = lax.axis_index("loop")
    depth = lax.axis_index("depth")
    z = loop // 8
    half = (loop // 4) % 2
    y = loop % 4
    node = loop // 4
    kind = (y - depth + 4) % 4
    first = depth == 0

    def remote(source, target, send, recv, device):
        return pltpu.make_async_remote_copy(
            src_ref=source, dst_ref=target, send_sem=send, recv_sem=recv, device_id=device, device_id_type=MESH
        )

    def toggled(value, bit):
        return value + bit - 2 * bit * ((value // bit) % 2)

    above = (((z + 1) % RING) * 8 + loop % 8, depth)
    below = (((z + RING - 1) % RING) * 8 + loop % 8, depth)
    mate_node = z * 2 + 1 - half
    mate_device = (mate_node * 4 + y, depth)
    team = [(node * 4 + (y + member) % 4, member) for member in range(4)]
    owners = [(node * 4 + kind, piece) for piece in range(4)]
    beside = [(loop, (depth + offset) % 4) for offset in range(1, 4)]
    two = (depth + 2) % 4

    def peer_device(member):
        return (node * 4 + (kind + member) % 4, member)

    def around(other):
        return (depth + 3 + 2 * other) % 4, (depth + 1 + 2 * other) % 4

    before = [(depth + 4 - offset) % 4 for offset in range(1, 4)]
    partners = [
        (toggled(loop, 32), depth), (toggled(loop, 16), depth), (toggled(loop, 8), depth), (toggled(loop, 2), depth),
        (toggled(loop, 1), depth), (toggled(loop, 4), depth), (loop, toggled(depth, 2)), (loop, toggled(depth, 1)),
    ]

    def section_of(slot):
        return ((loop - depth - kind - 4 * slot + 128) // 4) % SECTIONS

    def step_of(index):
        distance = (index + 2) // 4
        up = ((index + 2) // 2) % 2
        other = index % 2
        slot = ((z + RING - distance + 2 * distance * up) % RING) * 2 + (half + other) % 2
        passes = (index >= 2) & ((distance < 3) | ((distance == 3) & (other == up)))
        return distance, up, other, slot, passes

    barrier = pltpu.get_barrier_semaphore()
    for device in [above, below] + beside + [peer_device((depth + offset) % 4) for offset in range(1, 4)] + [mate_device, partners[0], partners[1], partners[3], partners[4]]:
        pl.semaphore_signal(barrier, inc=1, device_id=device, device_id_type=MESH)
    for index in range(4):
        def greet(index=index):
            pl.semaphore_signal(barrier, inc=1, device_id=team[index], device_id_type=MESH)
            pl.semaphore_signal(barrier, inc=1, device_id=owners[index], device_id_type=MESH)

        if index == 0:
            pl.when(jnp.logical_not(first))(greet)
        else:
            greet()

    order_row = lax.broadcasted_iota(jnp.int32, (TILE, TILE), 0)
    order_col = lax.broadcasted_iota(jnp.int32, (TILE, TILE), 1)
    order = jnp.where(order_col == 8 * (order_row % 16) + order_row // 16, 1.0, 0.0)
    norm_row = norm[...]
    norm_full = jnp.broadcast_to(norm_row, (FEAT, PIECE)).T
    scaled = (norm_full * features[...]).astype(jnp.bfloat16)
    for tile in range(2):
        own[pl.ds(tile * TILE, TILE), :] = jnp.dot(
            order.astype(jnp.bfloat16), scaled[tile * TILE:(tile + 1) * TILE], preferred_element_type=jnp.float32
        ).astype(jnp.bfloat16)

    pl.semaphore_wait(barrier, jnp.where(first, 19, 21))

    mine = pl.ds(pl.multiple_of(depth * PIECE, PIECE), PIECE)

    def team_copy(other, member):
        return remote(
            own if other == 0 else mate, stripes.at[node if other == 0 else mate_node, mine],
            team_send.at[other, member], team_recv.at[other, depth], team[member],
        )

    mate_copy = remote(own, mate, mate_send, mate_recv, mate_device)
    mate_copy.start()
    for other in range(2):
        if other == 1:
            mate_copy.wait_recv()
        for member in range(4):
            if member == 0:
                @pl.when(jnp.logical_not(first))
                def _(other=other):
                    team_copy(other, 0).start()
            else:
                team_copy(other, member).start()

    @pl.when(first)
    def _():
        stripes[node, 0:PIECE, :] = own[...]
        stripes[mate_node, 0:PIECE, :] = mate[...]

    totals[...] = jnp.zeros_like(totals)

    wide = pl.ds(0, WIDE)
    thin = pl.ds(pl.multiple_of(WIDE + TILE * depth, TILE), TILE)

    def ring_copy(slot, send, device):
        rows = stripes.at[slot, wide]
        return remote(rows, rows, send, ring_recv.at[slot], device)

    def thin_copy(slot, send, device):
        rows = stripes.at[slot, thin]
        return remote(rows, rows, send, thin_recv.at[slot], device)

    def quarter(slot, member):
        return stripes.at[slot, pl.ds(pl.multiple_of(WIDE + TILE * member, TILE), TILE)]

    def peer_copy(slot, member, which, target):
        rows = quarter(slot, member)
        return remote(rows, rows, peer_send.at[slot, which], peer_recv.at[slot, member], peer_device(target))

    def pass_on(index):
        distance, up, other, slot, passes = step_of(index)

        @pl.when(index < 2)
        def _():
            for piece in range(4):
                def arrived(piece=piece):
                    remote(
                        own, stripes.at[slot, pl.ds(piece * PIECE, PIECE)], team_send.at[0, 0],
                        team_recv.at[other, piece], above,
                    ).wait_recv()

                if piece == 0:
                    pl.when(jnp.logical_not(first))(arrived)
                else:
                    arrived()
            thin_copy(slot, thin_send.at[slot], above).start()
            thin_copy(slot, thin_send_low.at[other], below).start()
            ring_copy(slot, ring_send.at[slot], above).start()
            ring_copy(slot, ring_send_low.at[other], below).start()

        @pl.when(index >= 2)
        def _():
            thin_copy(slot, thin_send.at[slot], above).wait_recv()

        @pl.when(passes & (up == 0))
        def _():
            thin_copy(slot, thin_send.at[slot], above).start()

        @pl.when(passes & (up == 1))
        def _():
            thin_copy(slot, thin_send.at[slot], below).start()

        @pl.when(index >= 2)
        def _():
            near, far = around(other)
            peer_copy(slot, depth, 0, far).start()
            peer_copy(slot, depth, 1, near).start()
            ring_copy(slot, ring_send.at[slot], above).wait_recv()

        @pl.when(passes & (up == 0))
        def _():
            ring_copy(slot, ring_send.at[slot], above).start()

        @pl.when(passes & (up == 1))
        def _():
            ring_copy(slot, ring_send.at[slot], below).start()

    def forward_step(count, carry):
        @pl.when(count < SECTIONS)
        def _():
            pass_on(count)

        @pl.when((count >= 4) & (count < SECTIONS + 2))
        def _():
            distance, up, other, slot, passes = step_of(count - 2)
            near, far = around(other)
            relay = peer_copy(slot, near, 2, far)
            relay.wait_recv()
            relay.start()

        @pl.when((count == 1) | (count == 2) | (count >= LAG + 2))
        def _():
            index = count - jnp.where(count < LAG, 1, LAG)
            distance, up, other, slot, passes = step_of(index)
            section = section_of(slot)

            @pl.when(index >= 2)
            def _():
                near, far = around(other)
                peer_copy(slot, far, 0, near).wait_recv()
                peer_copy(slot, two, 0, near).wait_recv()

            totals[...] += jnp.dot(blocks[section], stripes[slot], preferred_element_type=jnp.float32)

        return carry

    lax.fori_loop(0, SECTIONS + LAG, forward_step, 0)

    twin, cross = toggled(depth, 1), toggled(depth, 2)

    def piece_of(member):
        return pl.ds(pl.multiple_of(member * PIECE, PIECE), PIECE)

    def part_copy(which):
        source = parting if which == 2 else totals.at[piece_of(toggled(twin, 2) if which == 1 else twin)]
        return remote(
            source, parts.at[which], part_send.at[which], part_recv.at[which], (loop, cross if which == 2 else twin)
        )

    part_copy(1).start()
    part_copy(0).start()
    part_copy(1).wait_recv()
    parting[...] = totals[piece_of(cross), :] + parts[1]
    part_copy(2).start()
    part_copy(0).wait_recv()
    summed = totals[mine, :] + parts[0]
    part_copy(2).wait_recv()
    summed = summed + parts[2]

    aggregated_b = (norm_full * summed).astype(jnp.bfloat16)
    pre = jnp.dot(aggregated_b, weight[...], preferred_element_type=jnp.float32)
    sigma = jax.nn.sigmoid(pre)
    act[...] = pre * sigma
    signal = (cotangent[...] * (sigma * (1.0 + pre * (1.0 - sigma)))).astype(jnp.bfloat16)
    backed = lax.dot_general(weight[...], signal, (((1,), (1,)), ((), ())), preferred_element_type=jnp.float32)
    own_pushed[...] = (norm_row * backed).astype(jnp.bfloat16)

    def push_copy(offset):
        return remote(
            own_pushed, pushed.at[:, mine], push_send.at[offset], push_recv.at[offset], beside[offset]
        )

    for offset in range(3):
        push_copy(offset).start()
    pushed[:, mine] = own_pushed[...]
    terms[0] = lax.dot_general(aggregated_b, signal, (((0,), (0,)), ((), ())), preferred_element_type=jnp.float32)

    def term_copy(step):
        return remote(terms.at[step], other_terms.at[step], term_send.at[step], term_recv.at[step], partners[step])

    term_copy(0).start()
    for offset in range(3):
        source = pl.ds(pl.multiple_of(before[offset] * PIECE, PIECE), PIECE)
        remote(
            own_pushed, pushed.at[:, source], push_send.at[offset], push_recv.at[offset], beside[offset]
        ).wait_recv()

    def share_copy(other, piece):
        return remote(
            shares.at[other, piece], shared.at[other, depth], share_send.at[other, piece], share_recv.at[other, depth],
            owners[piece],
        )

    def back_copy(slot, target, recv, device):
        return remote(going.at[slot], target, back_send.at[slot], recv, device)

    def back_thin_copy(slot, target, recv, device):
        return remote(going_thin.at[slot], target, back_thin_send.at[slot], recv, device)

    def give_copy(slot, which, target):
        return remote(
            given.at[slot, which], taken.at[slot, which], give_send.at[slot, which], give_recv.at[slot, which],
            peer_device(target),
        )

    def lanes_of(member):
        return pl.ds(pl.multiple_of(WIDE + TILE * member, TILE), TILE)

    def multiply(index, held):
        distance, up, other, slot, passes = step_of(index)
        sums[held] = jnp.dot(pushed[...], blocks[section_of(slot)], preferred_element_type=jnp.float32)

        @pl.when(index >= 2)
        def _():
            near, far = around(other)
            given[slot, 0] = sums[held, :, lanes_of(two)].astype(jnp.bfloat16)
            give_copy(slot, 0, near).start()
            given[slot, 2] = sums[held, :, lanes_of(far)].astype(jnp.bfloat16)
            give_copy(slot, 2, far).start()

    def hand_on(index, held):
        distance, up, other, slot, passes = step_of(index)
        near, far = around(other)
        give_copy(slot, 0, near).wait_recv()
        given[slot, 1] = (sums[held, :, lanes_of(near)] + taken[slot, 0].astype(jnp.float32)).astype(jnp.bfloat16)
        give_copy(slot, 1, near).start()

    def share(other, held, pieces):
        for piece in pieces:
            shares[other, piece] = sums[held, :, pl.ds(piece * PIECE, PIECE)].astype(jnp.bfloat16)
            if piece == 0:
                @pl.when(jnp.logical_not(first))
                def _():
                    share_copy(other, 0).start()

                @pl.when(first)
                def _():
                    shared[other, 0] = shares[other, 0]
            else:
                share_copy(other, piece).start()

    def send_back(index, copy, main, low):
        distance, up, other, slot, passes = step_of(index)
        last_far = distance == 4

        @pl.when((index >= 2) & (((up == 0) & jnp.logical_not(last_far)) | (last_far & (other == 0))))
        def _():
            copy(slot, main[0].at[slot], main[1].at[slot], below).start()

        @pl.when((index >= 2) & (((up == 1) & (distance > 1)) | (last_far & (other == 1))))
        def _():
            copy(slot, main[0].at[slot], main[1].at[slot], above).start()

        @pl.when((index >= 2) & (up == 1) & (distance == 1))
        def _():
            copy(slot, low[0].at[other], low[1].at[other], above).start()

    def reduce_wide(index, held):
        distance, up, other, slot, passes = step_of(index)

        @pl.when(passes | (index < 2))
        def _():
            back_copy(slot, coming.at[slot], back_recv.at[slot], above).wait_recv()
            sums[held, :, wide] += coming[slot].astype(jnp.float32)

        @pl.when(index < 2)
        def _():
            back_copy(slot, coming_low.at[other], back_recv_low.at[other], below).wait_recv()
            sums[held, :, wide] += coming_low[other].astype(jnp.float32)
            share(other, held, (0, 1))

        @pl.when(index >= 2)
        def _():
            going[slot] = sums[held, :, wide].astype(jnp.bfloat16)

        send_back(index, back_copy, (coming, back_recv), (coming_low, back_recv_low))

    def reduce_thin(index, held):
        distance, up, other, slot, passes = step_of(index)

        @pl.when(index >= 2)
        def _():
            near, far = around(other)
            for which in (1, 2):
                give_copy(slot, which, near).wait_recv()
                sums[held, :, thin] += taken[slot, which].astype(jnp.float32)

        @pl.when(passes | (index < 2))
        def _():
            back_thin_copy(slot, coming_thin.at[slot], back_thin_recv.at[slot], above).wait_recv()
            sums[held, :, thin] += coming_thin[slot].astype(jnp.float32)

        @pl.when(index < 2)
        def _():
            back_thin_copy(slot, coming_thin_low.at[other], back_thin_recv_low.at[other], below).wait_recv()
            sums[held, :, thin] += coming_thin_low[other].astype(jnp.float32)
            share(other, held, (2, 3))

        @pl.when(index >= 2)
        def _():
            going_thin[slot] = sums[held, :, thin].astype(jnp.bfloat16)

        send_back(index, back_thin_copy, (coming_thin, back_thin_recv), (coming_thin_low, back_thin_recv_low))

    def backward_step(count, carry):
        @pl.when(count < SECTIONS)
        def _():
            multiply(SECTIONS - 1 - count, count % (LAG + 1))

        @pl.when((count >= 1) & (count < SECTIONS + 1))
        def _():
            reduce_wide(SECTIONS - count, (count - 1) % (LAG + 1))

        @pl.when((count >= 2) & (count < SECTIONS))
        def _():
            hand_on(SECTIONS + 1 - count, (count - 2) % (LAG + 1))

        @pl.when(count >= LAG)
        def _():
            reduce_thin(SECTIONS - 1 - (count - LAG), (count - LAG) % (LAG + 1))

        for step in range(1, 8):
            @pl.when(count == (2, 4, 6, 9, 12, 15, 18)[step - 1])
            def _(step=step):
                term_copy(step - 1).wait_recv()
                terms[step] = terms[step - 1] + other_terms[step - 1]
                term_copy(step).start()

        return carry

    lax.fori_loop(0, SECTIONS + LAG, backward_step, 0)

    def shared_sum(other):
        gathered = jnp.zeros((FEAT, PIECE), jnp.float32)
        for member in range(4):
            def share_arrived(member=member):
                remote(
                    shares.at[0, 0], shared.at[other, member], share_send.at[0, 0], share_recv.at[other, member], above
                ).wait_recv()

            if member == 0:
                pl.when(jnp.logical_not(first))(share_arrived)
            else:
                share_arrived()
            gathered = gathered + shared[other, member].astype(jnp.float32)
        return gathered

    mate_out[...] = shared_sum(1).astype(jnp.bfloat16)
    mate_back = remote(mate_out, mate_in, mate_back_send, mate_back_recv, mate_device)
    mate_back.start()
    gathered = shared_sum(0)
    mate_back.wait_recv()
    gathered = gathered + mate_in[...].astype(jnp.float32)
    for tile in range(2):
        feature_grad[pl.ds(tile * TILE, TILE), :] = norm_full[tile * TILE:(tile + 1) * TILE] * lax.dot_general(
            order, gathered[:, tile * TILE:(tile + 1) * TILE], (((0,), (1,)), ((), ())),
            precision=lax.Precision.HIGHEST, preferred_element_type=jnp.float32,
        )

    term_copy(7).wait_recv()
    weight_grad[...] = terms[7] + other_terms[7]

    mate_copy.wait_send()
    mate_back.wait_send()
    for other in range(2):
        for index in range(4):
            def sent(other=other, index=index):
                team_copy(other, index).wait_send()
                share_copy(other, index).wait_send()

            if index == 0:
                pl.when(jnp.logical_not(first))(sent)
            else:
                sent()
    for offset in range(3):
        part_copy(offset).wait_send()
        push_copy(offset).wait_send()
    for step in range(8):
        term_copy(step).wait_send()

    def sent_step(index, carry):
        distance, up, other, slot, passes = step_of(index)

        @pl.when(index < 2)
        def _():
            ring_copy(slot, ring_send_low.at[other], below).wait_send()
            thin_copy(slot, thin_send_low.at[other], below).wait_send()

        @pl.when(passes | (index < 2))
        def _():
            ring_copy(slot, ring_send.at[slot], above).wait_send()
            thin_copy(slot, thin_send.at[slot], above).wait_send()

        @pl.when(index >= 2)
        def _():
            back_copy(slot, coming.at[slot], back_recv.at[slot], above).wait_send()
            back_thin_copy(slot, coming_thin.at[slot], back_thin_recv.at[slot], above).wait_send()
            for which in range(3):
                peer_copy(slot, depth, which, two).wait_send()
                give_copy(slot, which, two).wait_send()

        return carry

    lax.fori_loop(0, SECTIONS, sent_step, 0)


def finish_kernel(act, feature_grad, weight_grad, act_out, feature_out, weight_out):
    act_out[...] = act[...]
    feature_out[...] = feature_grad[...]
    weight_out[...] = weight_grad[...]


def finish(*results):
    vmem = pl.BlockSpec(memory_space=pltpu.VMEM)
    return pl.pallas_call(
        finish_kernel,
        out_shape=tuple(jax.ShapeDtypeStruct(value.shape, value.dtype) for value in results),
        in_specs=[vmem] * 3,
        out_specs=(vmem,) * 3,
        compiler_params=pltpu.CompilerParams(vmem_limit_bytes=60 * 1024 * 1024),
        cost_estimate=pl.CostEstimate(flops=0, bytes_accessed=640_000, transcendentals=0),
    )(*results)


def layer(features, norm_row, weight, cotangent, dense):
    vmem = pl.BlockSpec(memory_space=pltpu.VMEM)
    dma = pltpu.SemaphoreType.DMA
    bf16, f32 = jnp.bfloat16, jnp.float32
    return pl.pallas_call(
        layer_kernel,
        out_shape=(
            jax.ShapeDtypeStruct((PIECE, FEAT), f32),
            jax.ShapeDtypeStruct((PIECE, FEAT), f32),
            jax.ShapeDtypeStruct((FEAT, FEAT), f32),
        ),
        in_specs=[vmem, vmem, vmem, vmem, vmem],
        out_specs=(vmem, vmem, vmem),
        scratch_shapes=[
            pltpu.VMEM((SECTIONS, STRIPE, FEAT), bf16),
            pltpu.VMEM((PIECE, FEAT), bf16),
            pltpu.VMEM((PIECE, FEAT), bf16),
            pltpu.VMEM((FEAT, PIECE), bf16),
            pltpu.VMEM((FEAT, PIECE), bf16),
            pltpu.VMEM((STRIPE, FEAT), f32),
            pltpu.VMEM((PIECE, FEAT), f32),
            pltpu.VMEM((3, PIECE, FEAT), f32),
            pltpu.VMEM((FEAT, STRIPE), bf16),
            pltpu.VMEM((FEAT, PIECE), bf16),
            pltpu.VMEM((LAG + 1, FEAT, STRIPE), f32),
            pltpu.VMEM((SECTIONS, FEAT, WIDE), bf16),
            pltpu.VMEM((SECTIONS, FEAT, TILE), bf16),
            pltpu.VMEM((SECTIONS, FEAT, WIDE), bf16),
            pltpu.VMEM((SECTIONS, FEAT, TILE), bf16),
            pltpu.VMEM((2, FEAT, WIDE), bf16),
            pltpu.VMEM((2, FEAT, TILE), bf16),
            pltpu.VMEM((SECTIONS, 3, FEAT, TILE), bf16),
            pltpu.VMEM((SECTIONS, 3, FEAT, TILE), bf16),
            pltpu.VMEM((2, 4, FEAT, PIECE), bf16),
            pltpu.VMEM((2, 4, FEAT, PIECE), bf16),
            pltpu.VMEM((8, FEAT, FEAT), f32),
            pltpu.VMEM((8, FEAT, FEAT), f32),
            dma, dma, dma, dma,
            dma((2, 4)), dma((2, 4)), dma((SECTIONS,)), dma((2,)), dma((SECTIONS,)),
            dma((SECTIONS,)), dma((2,)), dma((SECTIONS,)), dma((SECTIONS, 3)), dma((SECTIONS, 4)),
            dma((3,)), dma((3,)), dma((3,)), dma((3,)),
            dma((SECTIONS,)), dma((SECTIONS,)), dma((2,)), dma((SECTIONS,)), dma((SECTIONS,)), dma((2,)),
            dma((SECTIONS, 3)), dma((SECTIONS, 3)),
            dma((2, 4)), dma((2, 4)), dma((8,)), dma((8,)),
        ],
        compiler_params=pltpu.CompilerParams(
            collective_id=0, has_side_effects=True, vmem_limit_bytes=30 * 1024 * 1024
        ),
        cost_estimate=pl.CostEstimate(flops=9_000_000_000, bytes_accessed=34_000_000, transcendentals=32768),
    )(features, norm_row, weight, cotangent, pltpu.with_memory_space_constraint(dense, pltpu.VMEM))


def per_device(features, norm_scale, weight, cotangent, tile_rows, tile_cols, tile_masks, tile_counts):
    dense = dense_blocks(tile_rows[0, 0], tile_cols[0, 0], tile_counts[0, 0], tile_masks[0, 0])
    return finish(*layer(features, norm_scale.reshape(1, -1), weight, cotangent, dense))


def solution(mesh):
    return jax.shard_map(
        per_device,
        mesh=mesh,
        in_specs=(
            P(("loop", "depth"), None),
            P(("loop", "depth")),
            P(),
            P(("loop", "depth"), None),
            P("loop", "depth", None, None),
            P("loop", "depth", None, None),
            P("loop", "depth", None, None, None),
            P("loop", "depth", None),
        ),
        out_specs=(P(("loop", "depth"), None), P(("loop", "depth"), None), P()),
        check_vma=False,
    )
```

```python
import jax
import jax.numpy as jnp
from jax import lax
from jax.experimental import pallas as pl
from jax.experimental.pallas import tpu as pltpu
from jax.sharding import PartitionSpec as P

TILE = 128
SECTIONS = 16
CAP = 48
STRIPE = 1024
PIECE = 256
FEAT = 128
RING = 8
UNROLL = 4
WIDE = 512
LAG = 4
MESH = pl.DeviceIdType.MESH


def dense_kernel(rows, cols, counts, masks, out, words, packed, sem):
    lane = lax.broadcasted_iota(jnp.int32, (8, 128), 1)
    row = lax.broadcasted_iota(jnp.int32, (8, 128), 0)
    place = row * 16 + lax.rem(lane, 16)
    bit = lax.div(lane, 16)

    def fetch(section, held):
        return pltpu.make_async_copy(masks.at[section], words.at[held], sem.at[held])

    fetch(0, 0).start()
    packed[pl.ds(CAP, UNROLL)] = jnp.zeros((UNROLL, 4, 128), jnp.int32)

    def near_of(group):
        return [
            jnp.take_along_axis(
                jnp.broadcast_to(packed[group * UNROLL + index, pl.ds(part, 1), :], (8, 128)),
                place, axis=1, mode="promise_in_bounds",
            )
            for index in range(UNROLL) for part in range(4)
        ]

    def section_step(section, carry):
        held = section % 2

        @pl.when(section + 1 < SECTIONS)
        def _():
            fetch(section + 1, (section + 1) % 2).start()

        out[section] = jnp.zeros((STRIPE, STRIPE), jnp.bfloat16)
        fetch(section, held).wait()
        for eight in range(CAP // 8):
            slots = pl.ds(eight * 8, 8)
            for part in range(4):
                value = words[held, slots, pl.ds(part * 512, 128)]
                for step in range(1, 4):
                    value = value | (words[held, slots, pl.ds(part * 512 + step * 128, 128)] << (8 * step))
                packed[slots, part, :] = value
        live_count = counts[section]

        def group_step(group, nears):
            later = near_of(group + 1)
            for index in range(UNROLL):
                slot = group * UNROLL + index
                live = jnp.where(slot < live_count, 1, 0)
                strips = [
                    ((nears[4 * index + part] >> (bit + 8 * step)) & live).astype(jnp.float32)
                    for part in range(4) for step in range(4)
                ]
                tile = jnp.concatenate(strips, axis=0).astype(jnp.bfloat16)
                top = pl.multiple_of(rows[section, slot] * TILE, TILE)
                left = pl.multiple_of(cols[section, slot] * TILE, TILE)
                out[section, pl.ds(top, TILE), pl.ds(left, TILE)] += tile
            return later

        lax.fori_loop(0, (live_count + UNROLL - 1) // UNROLL, group_step, near_of(0))
        return carry

    lax.fori_loop(0, SECTIONS, section_step, 0)


def dense_blocks(tile_rows, tile_cols, tile_counts, tile_masks):
    smem = pl.BlockSpec(memory_space=pltpu.SMEM)
    return pl.pallas_call(
        dense_kernel,
        out_shape=pltpu.VMEM((SECTIONS, STRIPE, STRIPE), jnp.bfloat16),
        in_specs=[smem, smem, smem, pl.BlockSpec(memory_space=pl.ANY)],
        out_specs=pl.BlockSpec(memory_space=pltpu.VMEM),
        scratch_shapes=[
            pltpu.VMEM((2, CAP, 2048), jnp.int32),
            pltpu.VMEM((CAP + UNROLL, 4, 128), jnp.int32),
            pltpu.SemaphoreType.DMA((2,)),
        ],
        compiler_params=pltpu.CompilerParams(vmem_limit_bytes=28 * 1024 * 1024),
        cost_estimate=pl.CostEstimate(flops=50_000_000, bytes_accessed=8_000_000, transcendentals=0),
    )(tile_rows, tile_cols, tile_counts, tile_masks)


def layer_kernel(
    features, norm, weight, cotangent, blocks, act, feature_grad, weight_grad,
    stripes, own, mate, mate_out, mate_in, totals, parting, parts, pushed, own_pushed, sums, going, going_thin, coming, coming_thin, coming_low,
    coming_thin_low, given, taken, shares, shared, terms, other_terms,
    mate_send, mate_recv, mate_back_send, mate_back_recv, team_send, team_recv, ring_send, ring_send_low, ring_recv, thin_send, thin_send_low, thin_recv, peer_send,
    peer_recv, part_send, part_recv, push_send, push_recv, back_send, back_recv, back_recv_low, back_thin_send,
    back_thin_recv, back_thin_recv_low, give_send, give_recv, share_send, share_recv, term_send, term_recv,
):
    loop = lax.axis_index("loop")
    depth = lax.axis_index("depth")
    z = loop // 8
    half = (loop // 4) % 2
    y = loop % 4
    node = loop // 4
    kind = (y - depth + 4) % 4
    first = depth == 0

    def remote(source, target, send, recv, device):
        return pltpu.make_async_remote_copy(
            src_ref=source, dst_ref=target, send_sem=send, recv_sem=recv, device_id=device, device_id_type=MESH
        )

    def toggled(value, bit):
        return value + bit - 2 * bit * ((value // bit) % 2)

    above = (((z + 1) % RING) * 8 + loop % 8, depth)
    below = (((z + RING - 1) % RING) * 8 + loop % 8, depth)
    mate_node = z * 2 + 1 - half
    mate_device = (mate_node * 4 + y, depth)
    team = [(node * 4 + (y + member) % 4, member) for member in range(4)]
    owners = [(node * 4 + kind, piece) for piece in range(4)]
    beside = [(loop, (depth + offset) % 4) for offset in range(1, 4)]
    two = (depth + 2) % 4

    def peer_device(member):
        return (node * 4 + (kind + member) % 4, member)

    def around(other):
        return (depth + 3 + 2 * other) % 4, (depth + 1 + 2 * other) % 4

    before = [(depth + 4 - offset) % 4 for offset in range(1, 4)]
    partners = [
        (toggled(loop, 32), depth), (toggled(loop, 16), depth), (toggled(loop, 8), depth), (toggled(loop, 2), depth),
        (toggled(loop, 1), depth), (toggled(loop, 4), depth), (loop, toggled(depth, 2)), (loop, toggled(depth, 1)),
    ]

    def section_of(slot):
        return ((loop - depth - kind - 4 * slot + 128) // 4) % SECTIONS

    def step_of(index):
        distance = (index + 2) // 4
        up = ((index + 2) // 2) % 2
        other = index % 2
        slot = ((z + RING - distance + 2 * distance * up) % RING) * 2 + (half + other) % 2
        passes = (index >= 2) & ((distance < 3) | ((distance == 3) & (other == up)))
        return distance, up, other, slot, passes

    barrier = pltpu.get_barrier_semaphore()
    for device in [above, below] + beside + [peer_device((depth + offset) % 4) for offset in range(1, 4)] + [mate_device, partners[0], partners[1], partners[3], partners[4]]:
        pl.semaphore_signal(barrier, inc=1, device_id=device, device_id_type=MESH)
    for index in range(4):
        def greet(index=index):
            pl.semaphore_signal(barrier, inc=1, device_id=team[index], device_id_type=MESH)
            pl.semaphore_signal(barrier, inc=1, device_id=owners[index], device_id_type=MESH)

        if index == 0:
            pl.when(jnp.logical_not(first))(greet)
        else:
            greet()

    order_row = lax.broadcasted_iota(jnp.int32, (TILE, TILE), 0)
    order_col = lax.broadcasted_iota(jnp.int32, (TILE, TILE), 1)
    order = jnp.where(order_col == 8 * (order_row % 16) + order_row // 16, 1.0, 0.0)
    norm_row = norm[...]
    norm_full = jnp.broadcast_to(norm_row, (FEAT, PIECE)).T
    scaled = (norm_full * features[...]).astype(jnp.bfloat16)
    for tile in range(2):
        own[pl.ds(tile * TILE, TILE), :] = jnp.dot(
            order.astype(jnp.bfloat16), scaled[tile * TILE:(tile + 1) * TILE], preferred_element_type=jnp.float32
        ).astype(jnp.bfloat16)

    pl.semaphore_wait(barrier, jnp.where(first, 19, 21))

    mine = pl.ds(pl.multiple_of(depth * PIECE, PIECE), PIECE)

    def team_copy(other, member):
        return remote(
            own if other == 0 else mate, stripes.at[node if other == 0 else mate_node, mine],
            team_send.at[other, member], team_recv.at[other, depth], team[member],
        )

    mate_copy = remote(own, mate, mate_send, mate_recv, mate_device)
    mate_copy.start()
    for other in range(2):
        if other == 1:
            mate_copy.wait_recv()
        for member in range(4):
            if member == 0:
                @pl.when(jnp.logical_not(first))
                def _(other=other):
                    team_copy(other, 0).start()
            else:
                team_copy(other, member).start()

    @pl.when(first)
    def _():
        stripes[node, 0:PIECE, :] = own[...]
        stripes[mate_node, 0:PIECE, :] = mate[...]

    totals[...] = jnp.zeros_like(totals)

    wide = pl.ds(0, WIDE)
    thin = pl.ds(pl.multiple_of(WIDE + TILE * depth, TILE), TILE)

    def ring_copy(slot, send, device):
        rows = stripes.at[slot, wide]
        return remote(rows, rows, send, ring_recv.at[slot], device)

    def thin_copy(slot, send, device):
        rows = stripes.at[slot, thin]
        return remote(rows, rows, send, thin_recv.at[slot], device)

    def quarter(slot, member):
        return stripes.at[slot, pl.ds(pl.multiple_of(WIDE + TILE * member, TILE), TILE)]

    def peer_copy(slot, member, which, target):
        rows = quarter(slot, member)
        return remote(rows, rows, peer_send.at[slot, which], peer_recv.at[slot, member], peer_device(target))

    def pass_on(index):
        distance, up, other, slot, passes = step_of(index)

        @pl.when(index < 2)
        def _():
            for piece in range(4):
                def arrived(piece=piece):
                    remote(
                        own, stripes.at[slot, pl.ds(piece * PIECE, PIECE)], team_send.at[0, 0],
                        team_recv.at[other, piece], above,
                    ).wait_recv()

                if piece == 0:
                    pl.when(jnp.logical_not(first))(arrived)
                else:
                    arrived()
            thin_copy(slot, thin_send.at[slot], above).start()
            thin_copy(slot, thin_send_low.at[other], below).start()
            ring_copy(slot, ring_send.at[slot], above).start()
            ring_copy(slot, ring_send_low.at[other], below).start()

        @pl.when(index >= 2)
        def _():
            thin_copy(slot, thin_send.at[slot], above).wait_recv()

        @pl.when(passes & (up == 0))
        def _():
            thin_copy(slot, thin_send.at[slot], above).start()

        @pl.when(passes & (up == 1))
        def _():
            thin_copy(slot, thin_send.at[slot], below).start()

        @pl.when(index >= 2)
        def _():
            near, far = around(other)
            peer_copy(slot, depth, 0, far).start()
            peer_copy(slot, depth, 1, near).start()
            ring_copy(slot, ring_send.at[slot], above).wait_recv()

        @pl.when(passes & (up == 0))
        def _():
            ring_copy(slot, ring_send.at[slot], above).start()

        @pl.when(passes & (up == 1))
        def _():
            ring_copy(slot, ring_send.at[slot], below).start()

    def forward_step(count, carry):
        @pl.when(count < SECTIONS)
        def _():
            pass_on(count)

        @pl.when((count >= 4) & (count < SECTIONS + 2))
        def _():
            distance, up, other, slot, passes = step_of(count - 2)
            near, far = around(other)
            relay = peer_copy(slot, near, 2, far)
            relay.wait_recv()
            relay.start()

        @pl.when((count == 1) | (count == 2) | (count >= LAG + 2))
        def _():
            index = count - jnp.where(count < LAG, 1, LAG)
            distance, up, other, slot, passes = step_of(index)
            section = section_of(slot)

            @pl.when(index >= 2)
            def _():
                near, far = around(other)
                peer_copy(slot, far, 0, near).wait_recv()
                peer_copy(slot, two, 0, near).wait_recv()

            totals[...] += jnp.dot(blocks[section], stripes[slot], preferred_element_type=jnp.float32)

        return carry

    lax.fori_loop(0, SECTIONS + LAG, forward_step, 0)

    twin, cross = toggled(depth, 1), toggled(depth, 2)

    def piece_of(member):
        return pl.ds(pl.multiple_of(member * PIECE, PIECE), PIECE)

    def part_copy(which):
        source = parting if which == 2 else totals.at[piece_of(toggled(twin, 2) if which == 1 else twin)]
        return remote(
            source, parts.at[which], part_send.at[which], part_recv.at[which], (loop, cross if which == 2 else twin)
        )

    part_copy(1).start()
    part_copy(0).start()
    part_copy(1).wait_recv()
    parting[...] = totals[piece_of(cross), :] + parts[1]
    part_copy(2).start()
    part_copy(0).wait_recv()
    summed = totals[mine, :] + parts[0]
    part_copy(2).wait_recv()
    summed = summed + parts[2]

    aggregated_b = (norm_full * summed).astype(jnp.bfloat16)
    pre = jnp.dot(aggregated_b, weight[...], preferred_element_type=jnp.float32)
    sigma = jax.nn.sigmoid(pre)
    act[...] = pre * sigma
    signal = (cotangent[...] * (sigma * (1.0 + pre * (1.0 - sigma)))).astype(jnp.bfloat16)
    backed = lax.dot_general(weight[...], signal, (((1,), (1,)), ((), ())), preferred_element_type=jnp.float32)
    own_pushed[...] = (norm_row * backed).astype(jnp.bfloat16)

    def push_copy(offset):
        return remote(
            own_pushed, pushed.at[:, mine], push_send.at[offset], push_recv.at[offset], beside[offset]
        )

    for offset in range(3):
        push_copy(offset).start()
    pushed[:, mine] = own_pushed[...]
    terms[0] = lax.dot_general(aggregated_b, signal, (((0,), (0,)), ((), ())), preferred_element_type=jnp.float32)

    def term_copy(step):
        return remote(terms.at[step], other_terms.at[step], term_send.at[step], term_recv.at[step], partners[step])

    term_copy(0).start()
    for offset in range(3):
        source = pl.ds(pl.multiple_of(before[offset] * PIECE, PIECE), PIECE)
        remote(
            own_pushed, pushed.at[:, source], push_send.at[offset], push_recv.at[offset], beside[offset]
        ).wait_recv()

    def share_copy(other, piece):
        return remote(
            shares.at[other, piece], shared.at[other, depth], share_send.at[other, piece], share_recv.at[other, depth],
            owners[piece],
        )

    def back_copy(slot, target, recv, device):
        return remote(going.at[slot], target, back_send.at[slot], recv, device)

    def back_thin_copy(slot, target, recv, device):
        return remote(going_thin.at[slot], target, back_thin_send.at[slot], recv, device)

    def give_copy(slot, which, target):
        return remote(
            given.at[slot, which], taken.at[slot, which], give_send.at[slot, which], give_recv.at[slot, which],
            peer_device(target),
        )

    def lanes_of(member):
        return pl.ds(pl.multiple_of(WIDE + TILE * member, TILE), TILE)

    def multiply(index, held):
        distance, up, other, slot, passes = step_of(index)
        section = section_of(slot)
        for part in range(4):
            lanes = pl.ds(part * 256, 256)
            sums[held, :, lanes] = jnp.dot(
                pushed[...], blocks[section, :, lanes], preferred_element_type=jnp.float32
            )

        @pl.when(index >= 2)
        def _():
            near, far = around(other)
            given[slot, 0] = sums[held, :, lanes_of(two)].astype(jnp.bfloat16)
            give_copy(slot, 0, near).start()
            given[slot, 2] = sums[held, :, lanes_of(far)].astype(jnp.bfloat16)
            give_copy(slot, 2, far).start()

    def hand_on(index, held):
        distance, up, other, slot, passes = step_of(index)
        near, far = around(other)
        give_copy(slot, 0, near).wait_recv()
        given[slot, 1] = (sums[held, :, lanes_of(near)] + taken[slot, 0].astype(jnp.float32)).astype(jnp.bfloat16)
        give_copy(slot, 1, near).start()

    def share(other, held, pieces):
        for piece in pieces:
            shares[other, piece] = sums[held, :, pl.ds(piece * PIECE, PIECE)].astype(jnp.bfloat16)
            if piece == 0:
                @pl.when(jnp.logical_not(first))
                def _():
                    share_copy(other, 0).start()

                @pl.when(first)
                def _():
                    shared[other, 0] = shares[other, 0]
            else:
                share_copy(other, piece).start()

    def send_back(index, copy, main, low):
        distance, up, other, slot, passes = step_of(index)
        last_far = distance == 4

        @pl.when((index >= 2) & (((up == 0) & jnp.logical_not(last_far)) | (last_far & (other == 0))))
        def _():
            copy(slot, main[0].at[slot], main[1].at[slot], below).start()

        @pl.when((index >= 2) & (((up == 1) & (distance > 1)) | (last_far & (other == 1))))
        def _():
            copy(slot, main[0].at[slot], main[1].at[slot], above).start()

        @pl.when((index >= 2) & (up == 1) & (distance == 1))
        def _():
            copy(slot, low[0].at[other], low[1].at[other], above).start()

    def reduce_wide(index, held):
        distance, up, other, slot, passes = step_of(index)

        @pl.when(passes | (index < 2))
        def _():
            back_copy(slot, coming.at[slot], back_recv.at[slot], above).wait_recv()
            sums[held, :, wide] += coming[slot].astype(jnp.float32)

        @pl.when(index < 2)
        def _():
            back_copy(slot, coming_low.at[other], back_recv_low.at[other], below).wait_recv()
            sums[held, :, wide] += coming_low[other].astype(jnp.float32)
            share(other, held, (0, 1))

        @pl.when(index >= 2)
        def _():
            going[slot] = sums[held, :, wide].astype(jnp.bfloat16)

        send_back(index, back_copy, (coming, back_recv), (coming_low, back_recv_low))

    def reduce_thin(index, held):
        distance, up, other, slot, passes = step_of(index)

        @pl.when(index >= 2)
        def _():
            near, far = around(other)
            for which in (1, 2):
                give_copy(slot, which, near).wait_recv()
                sums[held, :, thin] += taken[slot, which].astype(jnp.float32)

        @pl.when(passes | (index < 2))
        def _():
            back_thin_copy(slot, coming_thin.at[slot], back_thin_recv.at[slot], above).wait_recv()
            sums[held, :, thin] += coming_thin[slot].astype(jnp.float32)

        @pl.when(index < 2)
        def _():
            back_thin_copy(slot, coming_thin_low.at[other], back_thin_recv_low.at[other], below).wait_recv()
            sums[held, :, thin] += coming_thin_low[other].astype(jnp.float32)
            share(other, held, (2, 3))

        @pl.when(index >= 2)
        def _():
            going_thin[slot] = sums[held, :, thin].astype(jnp.bfloat16)

        send_back(index, back_thin_copy, (coming_thin, back_thin_recv), (coming_thin_low, back_thin_recv_low))

    def backward_step(count, carry):
        @pl.when(count < SECTIONS)
        def _():
            multiply(SECTIONS - 1 - count, count % (LAG + 1))

        @pl.when((count >= 1) & (count < SECTIONS + 1))
        def _():
            reduce_wide(SECTIONS - count, (count - 1) % (LAG + 1))

        @pl.when((count >= 2) & (count < SECTIONS))
        def _():
            hand_on(SECTIONS + 1 - count, (count - 2) % (LAG + 1))

        @pl.when(count >= LAG)
        def _():
            reduce_thin(SECTIONS - 1 - (count - LAG), (count - LAG) % (LAG + 1))

        for step in range(1, 8):
            @pl.when(count == (2, 4, 6, 9, 12, 15, 18)[step - 1])
            def _(step=step):
                term_copy(step - 1).wait_recv()
                terms[step] = terms[step - 1] + other_terms[step - 1]
                term_copy(step).start()

        return carry

    lax.fori_loop(0, SECTIONS + LAG, backward_step, 0)

    def shared_sum(other):
        gathered = jnp.zeros((FEAT, PIECE), jnp.float32)
        for member in range(4):
            def share_arrived(member=member):
                remote(
                    shares.at[0, 0], shared.at[other, member], share_send.at[0, 0], share_recv.at[other, member], above
                ).wait_recv()

            if member == 0:
                pl.when(jnp.logical_not(first))(share_arrived)
            else:
                share_arrived()
            gathered = gathered + shared[other, member].astype(jnp.float32)
        return gathered

    mate_out[...] = shared_sum(1).astype(jnp.bfloat16)
    mate_back = remote(mate_out, mate_in, mate_back_send, mate_back_recv, mate_device)
    mate_back.start()
    gathered = shared_sum(0)
    mate_back.wait_recv()
    gathered = gathered + mate_in[...].astype(jnp.float32)
    for tile in range(2):
        feature_grad[pl.ds(tile * TILE, TILE), :] = norm_full[tile * TILE:(tile + 1) * TILE] * lax.dot_general(
            order, gathered[:, tile * TILE:(tile + 1) * TILE], (((0,), (1,)), ((), ())),
            precision=lax.Precision.HIGHEST, preferred_element_type=jnp.float32,
        )

    term_copy(7).wait_recv()
    weight_grad[...] = terms[7] + other_terms[7]

    mate_copy.wait_send()
    mate_back.wait_send()
    for other in range(2):
        for index in range(4):
            def sent(other=other, index=index):
                team_copy(other, index).wait_send()
                share_copy(other, index).wait_send()

            if index == 0:
                pl.when(jnp.logical_not(first))(sent)
            else:
                sent()
    for offset in range(3):
        part_copy(offset).wait_send()
        push_copy(offset).wait_send()
    for step in range(8):
        term_copy(step).wait_send()

    def sent_step(index, carry):
        distance, up, other, slot, passes = step_of(index)

        @pl.when(index < 2)
        def _():
            ring_copy(slot, ring_send_low.at[other], below).wait_send()
            thin_copy(slot, thin_send_low.at[other], below).wait_send()

        @pl.when(passes | (index < 2))
        def _():
            ring_copy(slot, ring_send.at[slot], above).wait_send()
            thin_copy(slot, thin_send.at[slot], above).wait_send()

        @pl.when(index >= 2)
        def _():
            back_copy(slot, coming.at[slot], back_recv.at[slot], above).wait_send()
            back_thin_copy(slot, coming_thin.at[slot], back_thin_recv.at[slot], above).wait_send()
            for which in range(3):
                peer_copy(slot, depth, which, two).wait_send()
                give_copy(slot, which, two).wait_send()

        return carry

    lax.fori_loop(0, SECTIONS, sent_step, 0)


def finish_kernel(act, feature_grad, weight_grad, act_out, feature_out, weight_out):
    act_out[...] = act[...]
    feature_out[...] = feature_grad[...]
    weight_out[...] = weight_grad[...]


def finish(*results):
    vmem = pl.BlockSpec(memory_space=pltpu.VMEM)
    return pl.pallas_call(
        finish_kernel,
        out_shape=tuple(jax.ShapeDtypeStruct(value.shape, value.dtype) for value in results),
        in_specs=[vmem] * 3,
        out_specs=(vmem,) * 3,
        compiler_params=pltpu.CompilerParams(vmem_limit_bytes=60 * 1024 * 1024),
        cost_estimate=pl.CostEstimate(flops=0, bytes_accessed=640_000, transcendentals=0),
    )(*results)


def layer(features, norm_row, weight, cotangent, dense):
    vmem = pl.BlockSpec(memory_space=pltpu.VMEM)
    dma = pltpu.SemaphoreType.DMA
    bf16, f32 = jnp.bfloat16, jnp.float32
    return pl.pallas_call(
        layer_kernel,
        out_shape=(
            jax.ShapeDtypeStruct((PIECE, FEAT), f32),
            jax.ShapeDtypeStruct((PIECE, FEAT), f32),
            jax.ShapeDtypeStruct((FEAT, FEAT), f32),
        ),
        in_specs=[vmem, vmem, vmem, vmem, vmem],
        out_specs=(vmem, vmem, vmem),
        scratch_shapes=[
            pltpu.VMEM((SECTIONS, STRIPE, FEAT), bf16),
            pltpu.VMEM((PIECE, FEAT), bf16),
            pltpu.VMEM((PIECE, FEAT), bf16),
            pltpu.VMEM((FEAT, PIECE), bf16),
            pltpu.VMEM((FEAT, PIECE), bf16),
            pltpu.VMEM((STRIPE, FEAT), f32),
            pltpu.VMEM((PIECE, FEAT), f32),
            pltpu.VMEM((3, PIECE, FEAT), f32),
            pltpu.VMEM((FEAT, STRIPE), bf16),
            pltpu.VMEM((FEAT, PIECE), bf16),
            pltpu.VMEM((LAG + 1, FEAT, STRIPE), f32),
            pltpu.VMEM((SECTIONS, FEAT, WIDE), bf16),
            pltpu.VMEM((SECTIONS, FEAT, TILE), bf16),
            pltpu.VMEM((SECTIONS, FEAT, WIDE), bf16),
            pltpu.VMEM((SECTIONS, FEAT, TILE), bf16),
            pltpu.VMEM((2, FEAT, WIDE), bf16),
            pltpu.VMEM((2, FEAT, TILE), bf16),
            pltpu.VMEM((SECTIONS, 3, FEAT, TILE), bf16),
            pltpu.VMEM((SECTIONS, 3, FEAT, TILE), bf16),
            pltpu.VMEM((2, 4, FEAT, PIECE), bf16),
            pltpu.VMEM((2, 4, FEAT, PIECE), bf16),
            pltpu.VMEM((8, FEAT, FEAT), f32),
            pltpu.VMEM((8, FEAT, FEAT), f32),
            dma, dma, dma, dma,
            dma((2, 4)), dma((2, 4)), dma((SECTIONS,)), dma((2,)), dma((SECTIONS,)),
            dma((SECTIONS,)), dma((2,)), dma((SECTIONS,)), dma((SECTIONS, 3)), dma((SECTIONS, 4)),
            dma((3,)), dma((3,)), dma((3,)), dma((3,)),
            dma((SECTIONS,)), dma((SECTIONS,)), dma((2,)), dma((SECTIONS,)), dma((SECTIONS,)), dma((2,)),
            dma((SECTIONS, 3)), dma((SECTIONS, 3)),
            dma((2, 4)), dma((2, 4)), dma((8,)), dma((8,)),
        ],
        compiler_params=pltpu.CompilerParams(
            collective_id=0, has_side_effects=True, vmem_limit_bytes=30 * 1024 * 1024
        ),
        cost_estimate=pl.CostEstimate(flops=9_000_000_000, bytes_accessed=34_000_000, transcendentals=32768),
    )(features, norm_row, weight, cotangent, pltpu.with_memory_space_constraint(dense, pltpu.VMEM))


def per_device(features, norm_scale, weight, cotangent, tile_rows, tile_cols, tile_masks, tile_counts):
    dense = dense_blocks(tile_rows[0, 0], tile_cols[0, 0], tile_counts[0, 0], tile_masks[0, 0])
    return finish(*layer(features, norm_scale.reshape(1, -1), weight, cotangent, dense))


def solution(mesh):
    return jax.shard_map(
        per_device,
        mesh=mesh,
        in_specs=(
            P(("loop", "depth"), None),
            P(("loop", "depth")),
            P(),
            P(("loop", "depth"), None),
            P("loop", "depth", None, None),
            P("loop", "depth", None, None),
            P("loop", "depth", None, None, None),
            P("loop", "depth", None),
        ),
        out_specs=(P(("loop", "depth"), None), P(("loop", "depth"), None), P()),
        check_vma=False,
    )
```
